32 devices in a mesh: row: 8 (over z, y), band: 4 (over x, core).
Axes of the slice: x: 2, y: 2, z: 4, core: 2. Of those that a mesh axis runs over, the one named last changes fastest.
Arguments:
- nodes: float32 [8, 3, 512], P('row', None, 'band'), may hold values from -6 to 6
- segments: float32 [8, 6, 3072], P('row', None, 'band'), may hold values from -6 to 6
- circulation: float32 [8, 3072], P('row', 'band'), may hold values from -1 to 1
- upstream: int32 [8, 3], P('row'), may hold values from 0 to 3, as said below
- upstream_mask: int32 [8, 3], P('row'), may hold values from 0 to 1, as said below
Outputs:
- new_nodes: float32 [8, 3, 512], P('row', None, 'band')
- velocity_first: float32 [8, 3, 512], P('row', None, 'band')
The draws below stay inside these ranges and needn't reach their ends.
Inputs may be any that keep to these rules, and one draw needn't show every extreme that they name: `upstream`: each turbine's used entries come first and name distinct turbines of the previous downwind row of 4 turbines (turbine t lies in downwind row t // 4); unused entries are 0. `upstream_mask`: turbines of the first downwind row use no entries; the last turbine uses all three.
All inputs are finite; a program needn't handle non-finite values.
Results may differ from the reference program's by a relative error of at most 0.00014.
Values sent between devices are 32-bit elements; how exact they have to be, the bound alone decides.
No kernel may reach another device: no remote copies, remote signals or barrier semaphores. Data moves between devices by JAX's collectives and lax.ppermute only.
A program may use at most 64 MiB of HBM per device.

```python
import math
import jax
import jax.numpy as jnp
from jax import lax

FIL = 8
TPR = 4
TURBINES = 8
NODES = 512
SEGS = 3072


def upstream_tables(key):
    order_key = jax.random.fold_in(key, 101)
    count_key = jax.random.fold_in(key, 202)
    turbine = jnp.arange(TURBINES, dtype=jnp.int32)
    downwind = turbine // TPR
    columns = jnp.arange(TPR, dtype=jnp.int32)
    scores = jax.random.randint(order_key, (TURBINES, TPR), 0, 1 << 20) * TPR + columns[None, :]
    forced = (turbine[:, None] == TURBINES - 1) & (columns[None, :] == TPR - 1)
    scores = jnp.where(forced, -1, scores)
    chosen = jnp.argsort(scores, axis=1)[:, :3].astype(jnp.int32)
    sources = (downwind[:, None] - 1) * TPR + chosen
    counts = jax.random.randint(count_key, (TURBINES,), 0, 4)
    counts = jnp.where(turbine == TURBINES - 1, 3, counts)
    counts = jnp.where(downwind == 0, 0, counts)
    live_flags = (jnp.arange(3, dtype=jnp.int32)[None, :] < counts[:, None]).astype(jnp.int32)
    return (jnp.where(live_flags > 0, sources, 0).astype(jnp.int32), live_flags)


def draw_upstream(key, part):
    return upstream_tables(key)[0]


def draw_upstream_mask(key, part):
    return upstream_tables(key)[1]


def shard_levels(own_key, extent, cuts, low, high):
    factor_of = 1.0
    for axis_at, shards_of in cuts:
        draws = jax.random.uniform(jax.random.fold_in(jax.random.fold_in(own_key, 6), axis_at), (shards_of,), jnp.float32, low / len(cuts), high / len(cuts))
        factor_of = factor_of * jnp.repeat(jnp.exp(draws), extent[axis_at] // shards_of).reshape((-1,) + (1,) * (len(extent) - 1 - axis_at))
    return factor_of


def noise(key, shape, width, bound, cuts=(), held_as=jnp.bfloat16):
    values = width * jax.random.normal(key, shape, jnp.float32)
    if cuts:
        values = values * shard_levels(key, shape, cuts, -0.22, 0.18)
    return jnp.clip(values, -bound, bound).astype(held_as)


def setup_inputs(seed: int = 0) -> dict:
    keys = jax.random.split(jax.random.key(seed), 6)
    return {
        "nodes": noise(keys[0], (TURBINES, 3, NODES), 1.0, 6.0, ((0, 8), (2, 4)), jnp.float32),
        "segments": noise(keys[1], (TURBINES, 6, SEGS), 1.0, 6.0, ((0, 8), (2, 4)), jnp.float32),
        "circulation": noise(keys[2], (TURBINES, SEGS), (max(SEGS // 100, 1)) ** -0.5, 1.0, ((0, 8), (1, 4)), jnp.float32),
        "upstream": draw_upstream(jax.random.fold_in(keys[5], 71), 0),
        "upstream_mask": draw_upstream_mask(jax.random.fold_in(keys[5], 71), 0),
    }


CORE_SQUARE = 0.04
AGE_STEP = 0.25

def segment_piece(points, piece):
    rel_one = points[:, :, None] - piece[0:3, None, :]
    rel_two = points[:, :, None] - piece[3:6, None, :]
    cross_x = rel_one[1] * rel_two[2] - rel_one[2] * rel_two[1]
    cross_y = rel_one[2] * rel_two[0] - rel_one[0] * rel_two[2]
    cross_z = rel_one[0] * rel_two[1] - rel_one[1] * rel_two[0]
    norm_one = jnp.sqrt(lax.optimization_barrier(jnp.sum(rel_one * rel_one, axis=0)) + CORE_SQUARE)
    norm_two = jnp.sqrt(lax.optimization_barrier(jnp.sum(rel_two * rel_two, axis=0)) + CORE_SQUARE)
    inner = lax.optimization_barrier(jnp.sum(rel_one * rel_two, axis=0))
    product = norm_one * norm_two
    factor = piece[6][None, :] * (norm_one + norm_two) / (4.0 * math.pi * product * (product + inner))
    return jnp.stack([lax.optimization_barrier(jnp.sum(cross_x * factor, axis=1)), lax.optimization_barrier(jnp.sum(cross_y * factor, axis=1)), lax.optimization_barrier(jnp.sum(cross_z * factor, axis=1))])

def induce(points, block):
    columns = block.shape[1]
    piece_len = 256 if columns % 256 == 0 else columns
    pieces = block.reshape(7, columns // piece_len, piece_len).transpose(1, 0, 2)

    def accumulate(total, piece):
        return (total + segment_piece(points, piece), None)
    total, ignored = lax.scan(accumulate, jnp.zeros((3, points.shape[1]), jnp.float32), pieces)
    return total

def free_stream():
    return jnp.array([1.0, 0.0, 0.0], jnp.float32)[:, None]

def shifted_back(field):
    return jnp.concatenate([field[:, :FIL], field[:, :-FIL]], axis=1)

def reference(nodes, segments, circulation, upstream, upstream_mask):
    blocks = jnp.concatenate([segments, circulation[:, None, :]], axis=1)
    node_count = nodes.shape[2]
    is_root = jnp.arange(node_count) < FIL

    def one_turbine(turbine):
        points = nodes[turbine]
        listed = upstream[turbine]
        weights = upstream_mask[turbine].astype(points.dtype)

        def velocity(where_at):
            total = induce(where_at, blocks[turbine])
            for slot in range(3):
                total = total + weights[slot] * induce(where_at, blocks[listed[slot]])
            return total + free_stream()
        first = velocity(points)
        prev_one = shifted_back(points)
        prev_two = shifted_back(prev_one)
        first_prev = shifted_back(first)
        predicted = jnp.where(is_root[None, :], points, prev_one + AGE_STEP * 0.5 * (first_prev + first))
        second = velocity(predicted)
        second_prev = shifted_back(second)
        updated = prev_one + AGE_STEP * 0.25 * (first_prev + first + second_prev + second) - (points - 2.0 * prev_one + prev_two) / 6.0
        updated = jnp.where(is_root[None, :], points, updated)
        return (updated, first)
    new_nodes, velocity_first = lax.map(one_turbine, jnp.arange(TURBINES, dtype=jnp.int32))
    return (new_nodes, velocity_first)
```

```python
import functools
import math

import jax
import jax.numpy as jnp
from jax import lax
from jax.experimental import pallas as pl
from jax.experimental.pallas import tpu as pltpu
from jax.sharding import PartitionSpec as P

FIL = 8
CORE_SQUARE = 0.04
AGE_STEP = 0.25
LISTED = 3
TILE = 256
F32, BF16 = jnp.float32, jnp.bfloat16


def split(value):
    high = value.astype(BF16).astype(F32)
    rest = value - high
    middle = rest.astype(BF16).astype(F32)
    return high, middle, rest - middle


def point_factors(points, norms_row):
    count = points.shape[1]
    zeros = lambda rows: jnp.zeros((rows, count), F32)
    terms = split(-2.0 * points)
    squared = jnp.sum(points * points, axis=0, keepdims=True)
    rows = []
    for term in (0, 1, 2, 0, 1, 2, 0, 1):
        rows += [zeros(3), terms[term], zeros(2)] if norms_row else [terms[term], zeros(5)]
    one = jnp.ones((1, count), F32)
    for _ in range(3):
        rows += [zeros(1), one, zeros(6)] if norms_row else [one, zeros(7)]
    rows += [*split(squared), zeros(5)]
    return jnp.concatenate(rows, axis=0).T.astype(BF16)


def segment_factors(block):
    one = jnp.ones((1, block.shape[1]), F32)
    zero = jnp.zeros_like(one)
    start = [block[i : i + 1] for i in range(3)]
    end = [block[i : i + 1] for i in range(3, 6)]
    scale = block[6:7] * (0.5 / math.pi)
    along = [a - b for a, b in zip(start, end)]
    moment = [
        start[1] * end[2] - start[2] * end[1],
        start[2] * end[0] - start[0] * end[2],
        start[0] * end[1] - start[1] * end[0],
    ]
    square = lambda v: v[0] * v[0] + v[1] * v[1] + v[2] * v[2]
    norms = jnp.concatenate(
        [square(start) + CORE_SQUARE, square(end) + CORE_SQUARE] + [zero] * 6, axis=0
    )
    high, middle, low = split(block)
    constant = jnp.concatenate([one] * 3 + [zero] * 5, axis=0)
    distance = jnp.concatenate(
        [high, high, high, middle, middle, middle, low, low, *split(norms), constant], axis=0
    ).astype(BF16)
    weights = jnp.concatenate([scale * v for v in along + moment] + [zero] * 2, axis=0)
    cross = jnp.concatenate([*split(weights), jnp.zeros_like(weights)], axis=0).astype(BF16)
    return distance, cross, square(along) + 2.0 * CORE_SQUARE


def kernel(
    bands, group, upstream, mask, here, there, updated_ref, first_ref, distance, cross, length
):
    own = group
    seg_count = here.shape[2]
    wake_slots = group + 1
    row, band = lax.axis_index("row"), lax.axis_index("band")
    count = updated_ref.shape[2]
    total_points = count + 2 * FIL
    used = mask[0, 0] + mask[0, 1] + mask[0, 2]

    def part_ref(part):
        half = bands // 2
        return (here, part) if part < half else (there, part - half)

    def slot_of(wake):
        listed = jnp.where(wake == 1, upstream[0, 0], jnp.where(wake == 2, upstream[0, 1], upstream[0, 2]))
        position = lax.rem(listed, group) ^ lax.rem(row, group)
        return jnp.where(wake == 0, own, position)

    def block_of(part, slot):
        ref, at = part_ref(part)
        return ref[at * wake_slots + slot]

    def node_block(block):
        return jnp.concatenate(
            [block[7:8, i * count : (i + 1) * count] for i in range(3)], axis=0
        )

    points = node_block(here[own])
    before = jnp.zeros_like(points)
    for part in range(1, bands):
        flip = sum(bands >> (bit + 1) for bit in range(bands.bit_length()) if part >> bit & 1)
        before = jnp.where(band ^ flip == band - 1, node_block(block_of(part, own)), before)
    at_start = band == 0
    root = points[:, :FIL]
    halo = jnp.where(at_start, jnp.concatenate([root, root], axis=1), before[:, -2 * FIL :])
    extended = jnp.concatenate([halo, points], axis=1)

    def add_tile(factors, total, wake, offset):
        at = pl.ds(offset, TILE)
        squared = jnp.dot(factors, distance[wake, :, at], preferred_element_type=F32)
        squared_one, squared_two = squared[:total_points], squared[total_points:]
        inverse_one, inverse_two = lax.rsqrt(squared_one), lax.rsqrt(squared_two)
        norms = squared_one * inverse_one + squared_two * inverse_two
        factor = (inverse_one + inverse_two) * pltpu.reciprocal(
            norms * norms - length[wake, :, at], approx=True
        )
        high = factor.astype(BF16)
        low = (factor - high.astype(F32)).astype(BF16)
        weights = cross[wake, :, at]
        contract = (((1,), (1,)), ((), ()))
        return (
            total
            + lax.dot_general(weights, high, contract, preferred_element_type=F32)
            + lax.dot_general(weights, low, contract, preferred_element_type=F32)
        )

    def velocity(where_at, prepare):
        factors = jnp.concatenate(
            [point_factors(where_at, 0), point_factors(where_at, 1)], axis=0
        )

        def one_wake(wake, total):
            if prepare:
                slot = slot_of(wake)
                for part in range(bands):
                    at = pl.ds(part * seg_count, seg_count)
                    parts = segment_factors(block_of(part, slot))
                    distance[wake, :, at], cross[wake, :, at], length[wake, :, at] = parts
            for tile in range(bands * seg_count // TILE):
                total = add_tile(factors, total, wake, tile * TILE)
            return total

        total = lax.fori_loop(0, 1 + used, one_wake, jnp.zeros((32, total_points), F32))
        sums = total[0:8] + total[8:16] + total[16:24]
        x, y, z = where_at[0:1], where_at[1:2], where_at[2:3]
        dx, dy, dz = sums[0:1], sums[1:2], sums[2:3]
        return jnp.concatenate(
            [
                y * dz - z * dy + sums[3:4] + 1.0,
                z * dx - x * dz + sums[4:5],
                x * dy - y * dx + sums[5:6],
            ],
            axis=0,
        )

    def shifted(field):
        return jnp.concatenate([field[:, :FIL], field[:, :-FIL]], axis=1)

    lane = lax.broadcasted_iota(jnp.int32, (3, total_points), 1)
    first = velocity(extended, True)
    pair = first + shifted(first)
    previous = shifted(extended)
    kept = (lane < FIL) | (at_start & (lane >= 2 * FIL) & (lane < 3 * FIL))
    predicted = jnp.where(kept, extended, previous + AGE_STEP * 0.5 * pair)
    second = velocity(predicted, False)
    pair = pair + second + shifted(second)
    updated = (
        previous + AGE_STEP * 0.25 * pair - (extended - 2.0 * previous + shifted(previous)) / 6.0
    )
    updated = jnp.where(kept, extended, updated)
    updated_ref[0] = updated[:, 2 * FIL :]
    first_ref[0] = first[:, 2 * FIL :]


def local(nodes, segments, circulation, upstream, upstream_mask):
    rows, bands = lax.axis_size("row"), lax.axis_size("band")
    group = min(8, rows // 2)
    seg_count = segments.shape[2]
    count = nodes.shape[2]
    node_row = jnp.pad(nodes.reshape(1, 3 * count), ((0, 0), (0, seg_count - 3 * count)))
    own = jnp.concatenate([segments[0], circulation, node_row], axis=0)[None]

    wakes, bit = own, 1
    while bit < group // 2:
        route = [(i, i ^ bit) for i in range(rows - group)]
        wakes = jnp.concatenate([wakes, lax.ppermute(wakes, "row", route)])
        bit *= 2
    arrived = [
        lax.ppermute(wakes, "row", [(i, (i ^ flip) + group) for i in range(rows - group)])
        for flip in ((0, bit) if group > 1 else (0,))
    ]
    here = jnp.concatenate(arrived + [own])
    bit = bands // 2
    while bit > 1:
        route = [(i, i ^ bit) for i in range(bands)]
        here = jnp.concatenate([here, lax.ppermute(here, "band", route)])
        bit //= 2
    there = lax.ppermute(here, "band", [(i, i ^ 1) for i in range(bands)])

    whole = pl.BlockSpec(memory_space=pltpu.VMEM)
    scalars = pl.BlockSpec(memory_space=pltpu.SMEM)
    out = jax.ShapeDtypeStruct((1, 3, count), F32)
    segs = bands * seg_count
    return pl.pallas_call(
        functools.partial(kernel, bands, group),
        out_shape=(out, out),
        in_specs=[scalars, scalars, whole, whole],
        out_specs=(whole, whole),
        scratch_shapes=[
            pltpu.VMEM((1 + LISTED, 96, segs), BF16),
            pltpu.VMEM((1 + LISTED, 32, segs), BF16),
            pltpu.VMEM((1 + LISTED, 1, segs), F32),
        ],
        compiler_params=pltpu.CompilerParams(vmem_limit_bytes=32 * 2**20),
    )(upstream, upstream_mask, here, there)


def solution(mesh):
    placed = (
        P("row", None, "band"),
        P("row", None, "band"),
        P("row", "band"),
        P("row", None),
        P("row", None),
    )
    return jax.shard_map(
        local,
        mesh=mesh,
        in_specs=placed,
        out_specs=(P("row", None, "band"), P("row", None, "band")),
        check_vma=False,
    )
```

```python
import functools
import math

import jax
import jax.numpy as jnp
from jax import lax
from jax.experimental import pallas as pl
from jax.experimental.pallas import tpu as pltpu
from jax.sharding import PartitionSpec as P

FIL = 8
CORE_SQUARE = 0.04
AGE_STEP = 0.25
LISTED = 3
TILE = 256
TERMS = 96
SUMS = 32
F32, BF16 = jnp.float32, jnp.bfloat16
VMEM = pl.BlockSpec(memory_space=pltpu.VMEM)
SMEM = pl.BlockSpec(memory_space=pltpu.SMEM)
ANY = pl.BlockSpec(memory_space=pl.ANY)
PARAMS = pltpu.CompilerParams(vmem_limit_bytes=32 * 2**20)


def split(value):
    high = value.astype(BF16).astype(F32)
    rest = value - high
    middle = rest.astype(BF16).astype(F32)
    return high, middle, rest - middle


def point_factors(points):
    count = points.shape[1]
    zeros = lambda rows: jnp.zeros((rows, count), F32)
    terms = split(-2.0 * points)
    squared = split(jnp.sum(points * points, axis=0, keepdims=True))
    one = jnp.ones((1, count), F32)
    both = []
    for end in (False, True):
        rows = []
        for term in (0, 1, 2, 0, 1, 2, 0, 1):
            rows += [zeros(3), terms[term], zeros(2)] if end else [terms[term], zeros(5)]
        for _ in range(3):
            rows += [zeros(1), one, zeros(6)] if end else [one, zeros(7)]
        rows += [*squared, zeros(5)]
        both.append(jnp.concatenate(rows, axis=0).T.astype(BF16))
    return jnp.concatenate(both, axis=0)


def segment_factors(block):
    one = jnp.ones((1, block.shape[1]), F32)
    zero = jnp.zeros_like(one)
    start = [block[i : i + 1] for i in range(3)]
    end = [block[i : i + 1] for i in range(3, 6)]
    scale = block[6:7] * (0.5 / math.pi)
    along = [a - b for a, b in zip(start, end)]
    moment = [
        start[1] * end[2] - start[2] * end[1],
        start[2] * end[0] - start[0] * end[2],
        start[0] * end[1] - start[1] * end[0],
    ]
    square = lambda v: v[0] * v[0] + v[1] * v[1] + v[2] * v[2]
    norms = jnp.concatenate(
        [square(start) + CORE_SQUARE, square(end) + CORE_SQUARE] + [zero] * 6, axis=0
    )
    high, middle, low = split(block)
    constant = jnp.concatenate([one] * 3 + [zero] * 5, axis=0)
    distance = jnp.concatenate(
        [high, high, high, middle, middle, middle, low, low, *split(norms), constant], axis=0
    ).astype(BF16)
    weights = jnp.concatenate([scale * v for v in along + moment] + [zero] * 2, axis=0)
    cross = jnp.concatenate([*split(weights), jnp.zeros_like(weights)], axis=0).astype(BF16)
    return distance, cross, square(along) + 2.0 * CORE_SQUARE


def add_tile(factors, distance, cross, length, total):
    points = factors.shape[0] // 2
    squared = jnp.dot(factors, distance, preferred_element_type=F32)
    squared_one, squared_two = squared[:points], squared[points:]
    inverse_one, inverse_two = lax.rsqrt(squared_one), lax.rsqrt(squared_two)
    norms = squared_one * inverse_one + squared_two * inverse_two
    factor = (inverse_one + inverse_two) * pltpu.reciprocal(norms * norms - length, approx=True)
    high = factor.astype(BF16)
    low = (factor - high.astype(F32)).astype(BF16)
    contract = (((1,), (1,)), ((), ()))
    return (
        total
        + lax.dot_general(cross, high, contract, preferred_element_type=F32)
        + lax.dot_general(cross, low, contract, preferred_element_type=F32)
    )


def add_wake(factors, wake, held, total):
    for distance, cross, length in held:
        for tile in range(distance.shape[2] // TILE):
            at = pl.ds(tile * TILE, TILE)
            total = add_tile(
                factors, distance[wake, :, at], cross[wake, :, at], length[wake, :, at], total
            )
    return total


def prepare(blocks, buffers, wake):
    distance, cross, length = buffers
    for part, block in enumerate(blocks):
        size = block.shape[1]
        at = pl.ds(part * size, size)
        distance[wake, :, at], cross[wake, :, at], length[wake, :, at] = segment_factors(block)


def used_wakes(mask):
    return mask[0, 0] + mask[0, 1] + mask[0, 2]


def slot_of(upstream, wake, group):
    listed = jnp.where(wake == 0, upstream[0, 0], jnp.where(wake == 1, upstream[0, 1], upstream[0, 2]))
    return lax.rem(listed, group) ^ lax.rem(lax.axis_index("row"), group)


def velocity(where_at, total):
    sums = total[0:8] + total[8:16] + total[16:24]
    x, y, z = where_at[0:1], where_at[1:2], where_at[2:3]
    dx, dy, dz = sums[0:1], sums[1:2], sums[2:3]
    return jnp.concatenate(
        [
            y * dz - z * dy + sums[3:4] + 1.0,
            z * dx - x * dz + sums[4:5],
            x * dy - y * dx + sums[5:6],
        ],
        axis=0,
    )


def pack_kernel(nodes, segments, circulation, packed, semaphores):
    count = nodes.shape[2]
    copies = [
        (circulation, packed.at[6:7]),
        *[(segments.at[i], packed.at[i : i + 1]) for i in range(6)],
        *[(nodes.at[i], packed.at[7:8, i * count : (i + 1) * count]) for i in range(3)],
    ]
    packed[7:8] = jnp.zeros((1, packed.shape[1]), F32)
    started = [
        pltpu.make_async_copy(source, target, semaphores.at[i])
        for i, (source, target) in enumerate(copies)
    ]
    for copy in started:
        copy.start()
    for copy in started:
        copy.wait()


def own_kernel(count, here, there, extended_ref, factors_ref, distance, cross, length, total_ref):
    half = here.shape[0]
    bands = 2 * half
    blocks = [here[i] for i in range(half)] + [there[i] for i in range(half)]
    node_block = lambda block: jnp.concatenate(
        [block[7:8, i * count : (i + 1) * count] for i in range(3)], axis=0
    )
    band = lax.axis_index("band")
    points = node_block(blocks[0])
    root = points[:, :FIL]
    halo = jnp.concatenate([root, root], axis=1)
    for part in range(1, bands):
        flip = sum(bands >> (bit + 1) for bit in range(bands.bit_length()) if part >> bit & 1)
        halo = jnp.where(band ^ flip == band - 1, node_block(blocks[part])[:, -2 * FIL :], halo)
    extended = jnp.concatenate([halo, points], axis=1)
    extended_ref[...] = extended
    factors = point_factors(extended)
    factors_ref[...] = factors
    prepare(blocks, (distance, cross, length), 0)
    total_ref[...] = add_wake(factors, 0, [(distance, cross, length)], jnp.zeros(total_ref.shape, F32))


def stage_kernel(group, upstream, mask, blocks, factors_ref, before, distance, cross, length, total_ref):
    parts = blocks.shape[0] // group
    factors = factors_ref[...]

    def one_wake(wake, total):
        slot = slot_of(upstream, wake, group)
        prepare([blocks[part * group + slot] for part in range(parts)], (distance, cross, length), wake)
        return add_wake(factors, wake, [(distance, cross, length)], total)

    total_ref[...] = lax.fori_loop(0, used_wakes(mask), one_wake, before[...])


def last_kernel(group, stages, upstream, mask, blocks, extended_ref, factors_ref, before, *refs):
    own, earlier = refs[:3], [refs[3 * i : 3 * i + 3] for i in range(1, stages + 1)]
    updated_ref, first_ref, distance, cross, length, results, semaphores = refs[3 * stages + 3 :]
    parts = blocks.shape[0] // group
    used = used_wakes(mask)
    factors = factors_ref[...]
    newest = (distance, cross, length)

    def first_pass(wake, total):
        slot = slot_of(upstream, wake, group)
        prepare([blocks[part * group + slot] for part in range(parts)], newest, wake)
        return add_wake(factors, wake, [newest], total)

    extended = extended_ref[...]
    total = lax.fori_loop(0, used, first_pass, before[...])
    first = velocity(extended, total)
    results[0] = first[:, 2 * FIL :]
    send_first = [
        pltpu.make_async_copy(results.at[0, i : i + 1], first_ref.at[i], semaphores.at[0, i])
        for i in range(3)
    ]
    for copy in send_first:
        copy.start()

    def shifted(field):
        return jnp.concatenate([field[:, :FIL], field[:, :-FIL]], axis=1)

    lane = lax.broadcasted_iota(jnp.int32, extended.shape, 1)
    at_start = lax.axis_index("band") == 0
    kept = (lane < FIL) | (at_start & (lane >= 2 * FIL) & (lane < 3 * FIL))
    pair = first + shifted(first)
    previous = shifted(extended)
    predicted = jnp.where(kept, extended, previous + AGE_STEP * 0.5 * pair)
    moved = point_factors(predicted)
    total = add_wake(moved, 0, [own], jnp.zeros_like(total))
    total = lax.fori_loop(
        0, used, lambda wake, total: add_wake(moved, wake, [*earlier, newest], total), total
    )
    second = velocity(predicted, total)
    pair = pair + second + shifted(second)
    updated = (
        previous + AGE_STEP * 0.25 * pair - (extended - 2.0 * previous + shifted(previous)) / 6.0
    )
    results[1] = jnp.where(kept, extended, updated)[:, 2 * FIL :]
    send_updated = [
        pltpu.make_async_copy(results.at[1, i : i + 1], updated_ref.at[i], semaphores.at[1, i])
        for i in range(3)
    ]
    for copy in send_updated:
        copy.start()
    for copy in send_first + send_updated:
        copy.wait()


def buffers(wakes, segs):
    shapes = ((TERMS, segs), BF16), ((SUMS, segs), BF16), ((1, segs), F32)
    return [((wakes, *shape), dtype) for shape, dtype in shapes]


def outs(*specs):
    return tuple(jax.ShapeDtypeStruct(shape, dtype) for shape, dtype in specs)


def cost(points, segs):
    pairs = points * segs
    return pl.CostEstimate(flops=500 * pairs, bytes_accessed=400 * segs, transcendentals=3 * pairs)


def local(nodes, segments, circulation, upstream, upstream_mask):
    rows, bands = lax.axis_size("row"), lax.axis_size("band")
    group = min(8, rows // 2)
    seg_count = segments.shape[2]
    count = nodes.shape[2]
    points = count + 2 * FIL
    sums = ((SUMS, points), F32)

    own = pl.pallas_call(
        pack_kernel,
        out_shape=jax.ShapeDtypeStruct((8, seg_count), F32),
        in_specs=[ANY] * 3,
        out_specs=VMEM,
        scratch_shapes=[pltpu.SemaphoreType.DMA((10,))],
    )(nodes.transpose(1, 0, 2), segments.transpose(1, 0, 2), circulation)[None]

    wakes, bit = own, 1
    while bit < group // 2:
        route = [(i, i ^ bit) for i in range(rows - group)]
        wakes = jnp.concatenate([wakes, lax.ppermute(wakes, "row", route)])
        bit *= 2
    arrived = [
        lax.ppermute(wakes, "row", [(i, (i ^ flip) + group) for i in range(rows - group)])
        for flip in ((0, bit) if group > 1 else (0,))
    ]

    def across(blocks, bit):
        return lax.ppermute(blocks, "band", [(i, i ^ bit) for i in range(bands)])

    here, bit = own, bands // 2
    while bit > 1:
        here = jnp.concatenate([here, across(here, bit)])
        bit //= 2
    there = across(here, 1)
    segs = bands * seg_count
    extended, factors, *held = pl.pallas_call(
        functools.partial(own_kernel, count),
        out_shape=outs(((3, points), F32), ((2 * points, TERMS), BF16), *buffers(1, segs), sums),
        in_specs=[VMEM] * 2,
        out_specs=(VMEM,) * 6,
        compiler_params=PARAMS,
        cost_estimate=cost(points, segs),
    )(here, there)
    total = held.pop()

    *arrived, total = lax.optimization_barrier((*arrived, total))
    here = fresh = jnp.concatenate(arrived)
    bit = bands // 2
    stages = 0
    while bit:
        following = across(here, bit)
        new_segs = fresh.shape[0] // group * seg_count
        *prepared, total = pl.pallas_call(
            functools.partial(stage_kernel, group),
            out_shape=outs(*buffers(LISTED, new_segs), sums),
            in_specs=[SMEM] * 2 + [VMEM] * 3,
            out_specs=(VMEM,) * 4,
            compiler_params=PARAMS,
            cost_estimate=cost(points, LISTED * new_segs),
        )(upstream, upstream_mask, fresh, factors, total)
        held += prepared
        stages += 1
        if bit > 1:
            following, total = lax.optimization_barrier((following, total))
        here, fresh = jnp.concatenate([here, following]), following
        bit //= 2

    new_segs = fresh.shape[0] // group * seg_count
    out = ((3, 1, count), F32)
    updated, first = pl.pallas_call(
        functools.partial(last_kernel, group, stages),
        out_shape=outs(out, out),
        in_specs=[SMEM] * 2 + [VMEM] * (4 + 3 * (stages + 1)),
        out_specs=(ANY,) * 2,
        scratch_shapes=[
            *[pltpu.VMEM(shape, dtype) for shape, dtype in buffers(LISTED, new_segs)],
            pltpu.VMEM((2, 3, count), F32),
            pltpu.SemaphoreType.DMA((2, 3)),
        ],
        compiler_params=PARAMS,
        cost_estimate=cost(points, 4 * segs),
    )(upstream, upstream_mask, fresh, extended, factors, total, *held)
    return updated.transpose(1, 0, 2), first.transpose(1, 0, 2)


def solution(mesh):
    placed = (
        P("row", None, "band"),
        P("row", None, "band"),
        P("row", "band"),
        P("row", None),
        P("row", None),
    )
    return jax.shard_map(
        local,
        mesh=mesh,
        in_specs=placed,
        out_specs=(P("row", None, "band"), P("row", None, "band")),
        check_vma=False,
    )
```

```python
import functools
import math

import jax
import jax.numpy as jnp
from jax import lax
from jax.experimental import pallas as pl
from jax.experimental.pallas import tpu as pltpu
from jax.sharding import PartitionSpec as P

FIL = 8
CORE_SQUARE = 0.04
AGE_STEP = 0.25
LISTED = 3
TILE = 256
TERMS = 96
SUMS = 32
F32, BF16 = jnp.float32, jnp.bfloat16
VMEM = pl.BlockSpec(memory_space=pltpu.VMEM)
ANY = pl.BlockSpec(memory_space=pl.ANY)
PARAMS = pltpu.CompilerParams(vmem_limit_bytes=32 * 2**20)


def split(value):
    high = value.astype(BF16).astype(F32)
    rest = value - high
    middle = rest.astype(BF16).astype(F32)
    return high, middle, rest - middle


def point_factors(points):
    count = points.shape[1]
    zeros = lambda rows: jnp.zeros((rows, count), F32)
    terms = split(-2.0 * points)
    squared = split(jnp.sum(points * points, axis=0, keepdims=True))
    one = jnp.ones((1, count), F32)
    both = []
    for end in (False, True):
        rows = []
        for term in (0, 1, 2, 0, 1, 2, 0, 1):
            rows += [zeros(3), terms[term], zeros(2)] if end else [terms[term], zeros(5)]
        for _ in range(3):
            rows += [zeros(1), one, zeros(6)] if end else [one, zeros(7)]
        rows += [*squared, zeros(5)]
        both.append(jnp.concatenate(rows, axis=0).T.astype(BF16))
    return jnp.concatenate(both, axis=0)


def segment_factors(block):
    one = jnp.ones((1, block.shape[1]), F32)
    zero = jnp.zeros_like(one)
    start = [block[i : i + 1] for i in range(3)]
    end = [block[i : i + 1] for i in range(3, 6)]
    scale = block[6:7] * (0.5 / math.pi)
    along = [a - b for a, b in zip(start, end)]
    moment = [
        start[1] * end[2] - start[2] * end[1],
        start[2] * end[0] - start[0] * end[2],
        start[0] * end[1] - start[1] * end[0],
    ]
    square = lambda v: v[0] * v[0] + v[1] * v[1] + v[2] * v[2]
    norms = jnp.concatenate(
        [square(start) + CORE_SQUARE, square(end) + CORE_SQUARE] + [zero] * 6, axis=0
    )
    high, middle, low = split(block)
    constant = jnp.concatenate([one] * 3 + [zero] * 5, axis=0)
    distance = jnp.concatenate(
        [high, high, high, middle, middle, middle, low, low, *split(norms), constant], axis=0
    ).astype(BF16)
    weights = jnp.concatenate([scale * v for v in along + moment] + [zero] * 2, axis=0)
    cross = jnp.concatenate([*split(weights), jnp.zeros_like(weights)], axis=0).astype(BF16)
    return distance, cross, square(along) + 2.0 * CORE_SQUARE


def add_tile(factors, distance, cross, length, total):
    points = factors.shape[0] // 2
    squared = jnp.dot(factors, distance, preferred_element_type=F32)
    squared_one, squared_two = squared[:points], squared[points:]
    inverse_one, inverse_two = lax.rsqrt(squared_one), lax.rsqrt(squared_two)
    norms = squared_one * inverse_one + squared_two * inverse_two
    factor = (inverse_one + inverse_two) * pltpu.reciprocal(norms * norms - length, approx=True)
    high = factor.astype(BF16)
    low = (factor - high.astype(F32)).astype(BF16)
    contract = (((1,), (1,)), ((), ()))
    return (
        total
        + lax.dot_general(cross, high, contract, preferred_element_type=F32)
        + lax.dot_general(cross, low, contract, preferred_element_type=F32)
    )


def add_wake(factors, wake, held, total):
    for distance, cross, length in held:
        for tile in range(distance.shape[2] // TILE):
            at = pl.ds(tile * TILE, TILE)
            total = add_tile(
                factors, distance[wake, :, at], cross[wake, :, at], length[wake, :, at], total
            )
    return total


def prepare(blocks, buffers, wake):
    distance, cross, length = buffers
    for part, block in enumerate(blocks):
        size = block.shape[1]
        at = pl.ds(part * size, size)
        distance[wake, :, at], cross[wake, :, at], length[wake, :, at] = segment_factors(block)


def used_wakes(mask):
    return jnp.sum(mask[...])


def slot_of(upstream, wake, group):
    lane = lax.broadcasted_iota(jnp.int32, upstream.shape, 1)
    listed = jnp.sum(jnp.where(lane == wake, upstream[...], 0))
    return lax.rem(listed, group) ^ lax.rem(lax.axis_index("row"), group)


def velocity(where_at, total):
    sums = total[0:8] + total[8:16] + total[16:24]
    x, y, z = where_at[0:1], where_at[1:2], where_at[2:3]
    dx, dy, dz = sums[0:1], sums[1:2], sums[2:3]
    return jnp.concatenate(
        [
            y * dz - z * dy + sums[3:4] + 1.0,
            z * dx - x * dz + sums[4:5],
            x * dy - y * dx + sums[5:6],
        ],
        axis=0,
    )


def pack_kernel(nodes, segments, circulation, packed, semaphores):
    count = nodes.shape[2]
    copies = [
        (circulation, packed.at[6:7]),
        *[(segments.at[i], packed.at[i : i + 1]) for i in range(6)],
        *[(nodes.at[i], packed.at[7:8, i * count : (i + 1) * count]) for i in range(3)],
    ]
    packed[7:8] = jnp.zeros((1, packed.shape[1]), F32)
    started = [
        pltpu.make_async_copy(source, target, semaphores.at[i])
        for i, (source, target) in enumerate(copies)
    ]
    for copy in started:
        copy.start()
    for copy in started:
        copy.wait()


def own_kernel(count, here, there, extended_ref, factors_ref, distance, cross, length, total_ref):
    bands = 1 + there.shape[0]
    blocks = [here[0]] + [there[i] for i in range(bands - 1)]
    node_block = lambda block: jnp.concatenate(
        [block[7:8, i * count : (i + 1) * count] for i in range(3)], axis=0
    )
    band = lax.axis_index("band")
    points = node_block(blocks[0])
    root = points[:, :FIL]
    halo = jnp.concatenate([root, root], axis=1)
    for flip in range(1, bands):
        halo = jnp.where(band ^ flip == band - 1, node_block(blocks[flip])[:, -2 * FIL :], halo)
    extended = jnp.concatenate([halo, points], axis=1)
    extended_ref[...] = extended
    factors = point_factors(extended)
    factors_ref[...] = factors
    prepare(blocks, (distance, cross, length), 0)
    total_ref[...] = add_wake(factors, 0, [(distance, cross, length)], jnp.zeros(total_ref.shape, F32))


def near_kernel(group, upstream, mask, blocks, factors_ref, before, distance, cross, length, total_ref):
    low = group // 2
    factors = factors_ref[...]
    size = blocks.shape[2]
    view = tuple(ref.at[:, :, :size] for ref in (distance, cross, length))

    def one_wake(wake, total):
        slot = slot_of(upstream, wake, group)

        def add(total):
            prepare([blocks[slot // low]], view, wake)
            return add_wake(factors, wake, [view], total)

        return lax.cond(lax.rem(slot, low) == 0, add, lambda total: total, total)

    total_ref[...] = lax.fori_loop(0, used_wakes(mask), one_wake, before[...])


def far_kernel(
    group, parts, upstream, mask, far, factors_ref, before, *refs
):
    low = group // 2
    tops = group // low
    distance, cross, length, total_ref = refs[3:]
    factors = factors_ref[...]
    size = far.shape[2]
    view = lambda part: tuple(
        ref.at[:, :, part * size : (part + 1) * size] for ref in (distance, cross, length)
    )

    def one_wake(wake, total):
        slot = slot_of(upstream, wake, group)

        def add(part, total):
            at = (lax.rem(slot, low) * parts + part) * tops + slot // low - tops
            prepare([far[at]], view(part), wake)
            return add_wake(factors, wake, [view(part)], total)

        total = lax.cond(lax.rem(slot, low) == 0, lambda t: t, functools.partial(add, 0), total)
        for part in range(1, parts):
            total = add(part, total)
        return total

    total_ref[...] = lax.fori_loop(0, used_wakes(mask), one_wake, before[...])


def last_kernel(group, parts, upstream, mask, blocks, extended_ref, factors_ref, before, *refs):
    own, earlier = refs[:3], refs[3:6]
    updated_ref, first_ref, distance, cross, length, results, semaphores = refs[6:]
    low = group // 2
    tops = group // low
    used = used_wakes(mask)
    factors = factors_ref[...]
    newest = (distance, cross, length)

    def first_pass(wake, total):
        slot = slot_of(upstream, wake, group)
        at = lambda part: (lax.rem(slot, low) * parts + part) * tops + slot // low
        prepare([blocks[at(part)] for part in range(parts)], newest, wake)
        return add_wake(factors, wake, [newest], total)

    extended = extended_ref[...]
    total = lax.fori_loop(0, used, first_pass, before[...])
    first = velocity(extended, total)
    results[0] = first[:, 2 * FIL :]
    send_first = [
        pltpu.make_async_copy(results.at[0, i : i + 1], first_ref.at[i], semaphores.at[0, i])
        for i in range(3)
    ]
    for copy in send_first:
        copy.start()

    def shifted(field):
        return jnp.concatenate([field[:, :FIL], field[:, :-FIL]], axis=1)

    lane = lax.broadcasted_iota(jnp.int32, extended.shape, 1)
    at_start = lax.axis_index("band") == 0
    kept = (lane < FIL) | (at_start & (lane >= 2 * FIL) & (lane < 3 * FIL))
    pair = first + shifted(first)
    previous = shifted(extended)
    predicted = jnp.where(kept, extended, previous + AGE_STEP * 0.5 * pair)
    moved = point_factors(predicted)
    total = add_wake(moved, 0, [own], jnp.zeros_like(total))
    total = lax.fori_loop(
        0, used, lambda wake, total: add_wake(moved, wake, [earlier, newest], total), total
    )
    second = velocity(predicted, total)
    pair = pair + second + shifted(second)
    updated = (
        previous + AGE_STEP * 0.25 * pair - (extended - 2.0 * previous + shifted(previous)) / 6.0
    )
    results[1] = jnp.where(kept, extended, updated)[:, 2 * FIL :]
    send_updated = [
        pltpu.make_async_copy(results.at[1, i : i + 1], updated_ref.at[i], semaphores.at[1, i])
        for i in range(3)
    ]
    for copy in send_updated:
        copy.start()
    for copy in send_first + send_updated:
        copy.wait()


def buffers(wakes, segs):
    shapes = ((TERMS, segs), BF16), ((SUMS, segs), BF16), ((1, segs), F32)
    return [((wakes, *shape), dtype) for shape, dtype in shapes]


def outs(*specs):
    return tuple(jax.ShapeDtypeStruct(shape, dtype) for shape, dtype in specs)


def cost(points, segs):
    pairs = points * segs
    return pl.CostEstimate(flops=500 * pairs, bytes_accessed=400 * segs, transcendentals=3 * pairs)


def local(nodes, segments, circulation, upstream, upstream_mask):
    rows, bands = lax.axis_size("row"), lax.axis_size("band")
    group = min(8, rows // 2)
    seg_count = segments.shape[2]
    count = nodes.shape[2]
    points = count + 2 * FIL
    sums = ((SUMS, points), F32)

    own = pl.pallas_call(
        pack_kernel,
        out_shape=pltpu.VMEM((8, seg_count), F32),
        in_specs=[ANY] * 3,
        out_specs=VMEM,
        scratch_shapes=[pltpu.SemaphoreType.DMA((10,))],
    )(nodes.transpose(1, 0, 2), segments.transpose(1, 0, 2), circulation)[None]

    low, parts = group // 2, bands // 2
    tops = group // low
    def across(blocks, bit):
        return lax.ppermute(blocks, "band", [(i, i ^ bit) for i in range(bands)])

    there = jnp.concatenate([across(own, flip) for flip in range(1, bands)])
    near = [
        lax.ppermute(own, "row", [(i, (i ^ flip) + group) for i in range(rows - group)])
        for flip in range(0, group, low)
    ]

    segs = bands * seg_count
    extended, factors, *held, total = pl.pallas_call(
        functools.partial(own_kernel, count),
        out_shape=outs(((3, points), F32), ((2 * points, TERMS), BF16), *buffers(1, segs), sums),
        in_specs=[VMEM] * 2,
        out_specs=(VMEM,) * 6,
        compiler_params=PARAMS,
        cost_estimate=cost(1, 1),
    )(own, there)

    *near, total = lax.optimization_barrier((*near, total))
    near = jnp.concatenate(near)

    def route(row_flip, band_flip):
        return [
            (i * bands + j, (i ^ row_flip) * bands + (j ^ 2 * band_flip))
            for i in range(group, rows)
            for j in range(bands)
        ]

    far = jnp.concatenate(
        [
            lax.ppermute(near, ("row", "band"), route(row_flip, band_flip))
            for row_flip in range(low)
            for band_flip in range(parts)
            if row_flip or band_flip
        ]
    )
    *half, total = pl.pallas_call(
        functools.partial(near_kernel, group),
        out_shape=outs(*buffers(LISTED, parts * seg_count), sums),
        in_specs=[VMEM] * 5,
        out_specs=(VMEM,) * 4,
        compiler_params=PARAMS,
        cost_estimate=cost(points, LISTED * seg_count),
    )(upstream, upstream_mask, near, factors, total)
    far, total = lax.optimization_barrier((far, total))
    last = across(jnp.concatenate([near, far]), 1)
    *half, total = pl.pallas_call(
        functools.partial(far_kernel, group, parts),
        out_shape=outs(*buffers(LISTED, parts * seg_count), sums),
        in_specs=[VMEM] * 8,
        out_specs=(VMEM,) * 4,
        input_output_aliases={5: 0, 6: 1, 7: 2},
        compiler_params=PARAMS,
        cost_estimate=cost(points, LISTED * seg_count),
    )(upstream, upstream_mask, far, factors, total, *half)

    out = ((3, 1, count), F32)
    updated, first = pl.pallas_call(
        functools.partial(last_kernel, group, parts),
        out_shape=outs(out, out),
        in_specs=[VMEM] * 12,
        out_specs=(ANY,) * 2,
        scratch_shapes=[
            *[pltpu.VMEM(shape, dtype) for shape, dtype in buffers(LISTED, parts * seg_count)],
            pltpu.VMEM((2, 3, count), F32),
            pltpu.SemaphoreType.DMA((2, 3)),
        ],
        compiler_params=PARAMS,
        cost_estimate=cost(points, 4 * segs),
    )(upstream, upstream_mask, last, extended, factors, total, *held, *half)
    return updated.transpose(1, 0, 2), first.transpose(1, 0, 2)


def solution(mesh):
    placed = (
        P("row", None, "band"),
        P("row", None, "band"),
        P("row", "band"),
        P("row", None),
        P("row", None),
    )
    return jax.shard_map(
        local,
        mesh=mesh,
        in_specs=placed,
        out_specs=(P("row", None, "band"), P("row", None, "band")),
        check_vma=False,
    )
```

```python
import functools
import math

import jax
import jax.numpy as jnp
from jax import lax
from jax.experimental import pallas as pl
from jax.experimental.pallas import tpu as pltpu
from jax.sharding import PartitionSpec as P

FIL = 8
CORE_SQUARE = 0.04
AGE_STEP = 0.25
LISTED = 3
TILE = 256
TERMS = 96
SUMS = 32
F32, BF16 = jnp.float32, jnp.bfloat16
VMEM = pl.BlockSpec(memory_space=pltpu.VMEM)
ANY = pl.BlockSpec(memory_space=pl.ANY)
PARAMS = pltpu.CompilerParams(vmem_limit_bytes=32 * 2**20)


def split(value):
    high = value.astype(BF16).astype(F32)
    rest = value - high
    middle = rest.astype(BF16).astype(F32)
    return high, middle, rest - middle


def point_factors(points):
    count = points.shape[1]
    zeros = lambda rows: jnp.zeros((rows, count), F32)
    terms = split(-2.0 * points)
    squared = split(jnp.sum(points * points, axis=0, keepdims=True))
    one = jnp.ones((1, count), F32)
    both = []
    for end in (False, True):
        rows = []
        for term in (0, 1, 2, 0, 1, 2, 0, 1):
            rows += [zeros(3), terms[term], zeros(2)] if end else [terms[term], zeros(5)]
        for _ in range(3):
            rows += [zeros(1), one, zeros(6)] if end else [one, zeros(7)]
        rows += [*squared, zeros(5)]
        both.append(jnp.concatenate(rows, axis=0).T.astype(BF16))
    return jnp.concatenate(both, axis=0)


def segment_factors(block):
    one = jnp.ones((1, block.shape[1]), F32)
    zero = jnp.zeros_like(one)
    start = [block[i : i + 1] for i in range(3)]
    end = [block[i : i + 1] for i in range(3, 6)]
    scale = block[6:7] * (0.5 / math.pi)
    along = [a - b for a, b in zip(start, end)]
    moment = [
        start[1] * end[2] - start[2] * end[1],
        start[2] * end[0] - start[0] * end[2],
        start[0] * end[1] - start[1] * end[0],
    ]
    square = lambda v: v[0] * v[0] + v[1] * v[1] + v[2] * v[2]
    norms = jnp.concatenate(
        [square(start) + CORE_SQUARE, square(end) + CORE_SQUARE] + [zero] * 6, axis=0
    )
    high, middle, low = split(block)
    constant = jnp.concatenate([one] * 3 + [zero] * 5, axis=0)
    distance = jnp.concatenate(
        [high, high, high, middle, middle, middle, low, low, *split(norms), constant], axis=0
    ).astype(BF16)
    weights = jnp.concatenate([scale * v for v in along + moment] + [zero] * 2, axis=0)
    cross = jnp.concatenate([*split(weights), jnp.zeros_like(weights)], axis=0).astype(BF16)
    return distance, cross, square(along) + 2.0 * CORE_SQUARE


def add_tile(factors, distance, cross, length, total):
    points = factors.shape[0] // 2
    squared = jnp.dot(factors, distance, preferred_element_type=F32)
    squared_one, squared_two = squared[:points], squared[points:]
    inverse_one, inverse_two = lax.rsqrt(squared_one), lax.rsqrt(squared_two)
    norms = squared_one * inverse_one + squared_two * inverse_two
    factor = (inverse_one + inverse_two) * pltpu.reciprocal(norms * norms - length, approx=True)
    high = factor.astype(BF16)
    low = (factor - high.astype(F32)).astype(BF16)
    contract = (((1,), (1,)), ((), ()))
    return (
        total
        + lax.dot_general(cross, high, contract, preferred_element_type=F32)
        + lax.dot_general(cross, low, contract, preferred_element_type=F32)
    )


def add_wake(factors, wake, held, total):
    for distance, cross, length in held:
        for tile in range(distance.shape[2] // TILE):
            at = pl.ds(tile * TILE, TILE)
            total = add_tile(
                factors, distance[wake, :, at], cross[wake, :, at], length[wake, :, at], total
            )
    return total


def prepare(blocks, buffers, wake):
    distance, cross, length = buffers
    for part, block in enumerate(blocks):
        size = block.shape[1]
        at = pl.ds(part * size, size)
        distance[wake, :, at], cross[wake, :, at], length[wake, :, at] = segment_factors(block)


def view_of(buffers, start, size):
    return tuple(ref.at[:, :, start : start + size] for ref in buffers)


def used_wakes(mask):
    return jnp.sum(mask[...])


def slot_of(upstream, wake, group):
    lane = lax.broadcasted_iota(jnp.int32, upstream.shape, 1)
    listed = jnp.sum(jnp.where(lane == wake, upstream[...], 0))
    return lax.rem(listed, group) ^ lax.rem(lax.axis_index("row"), group)


def velocity(where_at, total):
    sums = total[0:8] + total[8:16] + total[16:24]
    x, y, z = where_at[0:1], where_at[1:2], where_at[2:3]
    dx, dy, dz = sums[0:1], sums[1:2], sums[2:3]
    return jnp.concatenate(
        [
            y * dz - z * dy + sums[3:4] + 1.0,
            z * dx - x * dz + sums[4:5],
            x * dy - y * dx + sums[5:6],
        ],
        axis=0,
    )


def pack_kernel(nodes, segments, circulation, packed, semaphores):
    count = nodes.shape[2]
    copies = [
        (circulation, packed.at[6:7]),
        *[(segments.at[i], packed.at[i : i + 1]) for i in range(6)],
        *[(nodes.at[i], packed.at[7:8, i * count : (i + 1) * count]) for i in range(3)],
    ]
    packed[7:8] = jnp.zeros((1, packed.shape[1]), F32)
    started = [
        pltpu.make_async_copy(source, target, semaphores.at[i])
        for i, (source, target) in enumerate(copies)
    ]
    for copy in started:
        copy.start()
    for copy in started:
        copy.wait()


def own_kernel(count, own, behind, extended_ref, factors_ref, distance, cross, length, total_ref):
    node_block = lambda block: jnp.concatenate(
        [block[7:8, i * count : (i + 1) * count] for i in range(3)], axis=0
    )
    points = node_block(own[0])
    root = points[:, :FIL]
    at_start = lax.axis_index("band") == 0
    halo = jnp.where(
        at_start, jnp.concatenate([root, root], axis=1), node_block(behind[0])[:, -2 * FIL :]
    )
    extended = jnp.concatenate([halo, points], axis=1)
    extended_ref[...] = extended
    factors = point_factors(extended)
    factors_ref[...] = factors
    view = view_of((distance, cross, length), 0, 2 * own.shape[2])
    prepare([own[0], behind[0]], view, 0)
    total_ref[...] = add_wake(factors, 0, [view], jnp.zeros(total_ref.shape, F32))


def near_kernel(group, upstream, mask, blocks, factors_ref, before, distance, cross, length, total_ref):
    low = group // 2
    factors = factors_ref[...]
    size = blocks.shape[2]
    view = view_of((distance, cross, length), 0, size)

    def one_wake(wake, total):
        slot = slot_of(upstream, wake, group)

        def add(total):
            prepare([blocks[slot // low]], view, wake)
            return add_wake(factors, wake, [view], total)

        return lax.cond(lax.rem(slot, low) == 0, add, lambda total: total, total)

    total_ref[...] = lax.fori_loop(0, used_wakes(mask), one_wake, before[...])


def far_kernel(group, parts, upstream, mask, far, own, factors_ref, before, *refs):
    low = group // 2
    tops = group // low
    listed, wake_own, total_ref = refs[6:9], refs[9:12], refs[12]
    factors = factors_ref[...]
    size = far.shape[2]
    view = lambda part: view_of(listed, part * size, size)

    def one_wake(wake, total):
        slot = slot_of(upstream, wake, group)

        def add(part, total):
            at = (lax.rem(slot, low) * parts + part) * tops + slot // low - tops
            prepare([far[at]], view(part), wake)
            return add_wake(factors, wake, [view(part)], total)

        total = lax.cond(lax.rem(slot, low) == 0, lambda t: t, functools.partial(add, 0), total)
        for part in range(1, parts):
            total = add(part, total)
        return total

    view_own = view_of(wake_own, 2 * size, size)
    prepare([own[0]], view_own, 0)
    total = add_wake(factors, 0, [view_own], before[...])
    total_ref[...] = lax.fori_loop(0, used_wakes(mask), one_wake, total)


def last_kernel(group, parts, upstream, mask, blocks, extended_ref, factors_ref, before, *refs):
    own, earlier = refs[:3], refs[3:6]
    updated_ref, first_ref = refs[6:8]
    newest, newest_own = refs[8:11], refs[11:14]
    results, semaphores = refs[14:]
    low = group // 2
    tops = group // low
    used = used_wakes(mask)
    factors = factors_ref[...]
    rest = blocks.shape[0] - 2 + lax.rem(lax.axis_index("band"), 2)
    prepare([blocks[rest]], newest_own, 0)

    def first_pass(wake, total):
        slot = slot_of(upstream, wake, group)
        at = lambda part: (lax.rem(slot, low) * parts + part) * tops + slot // low
        prepare([blocks[at(part)] for part in range(parts)], newest, wake)
        return add_wake(factors, wake, [newest], total)

    extended = extended_ref[...]
    total = add_wake(factors, 0, [newest_own], before[...])
    total = lax.fori_loop(0, used, first_pass, total)
    first = velocity(extended, total)
    results[0] = first[:, 2 * FIL :]
    send_first = [
        pltpu.make_async_copy(results.at[0, i : i + 1], first_ref.at[i], semaphores.at[0, i])
        for i in range(3)
    ]
    for copy in send_first:
        copy.start()

    def shifted(field):
        return jnp.concatenate([field[:, :FIL], field[:, :-FIL]], axis=1)

    lane = lax.broadcasted_iota(jnp.int32, extended.shape, 1)
    at_start = lax.axis_index("band") == 0
    kept = (lane < FIL) | (at_start & (lane >= 2 * FIL) & (lane < 3 * FIL))
    pair = first + shifted(first)
    previous = shifted(extended)
    predicted = jnp.where(kept, extended, previous + AGE_STEP * 0.5 * pair)
    moved = point_factors(predicted)
    total = add_wake(moved, 0, [own, newest_own], jnp.zeros_like(total))
    total = lax.fori_loop(
        0, used, lambda wake, total: add_wake(moved, wake, [earlier, newest], total), total
    )
    second = velocity(predicted, total)
    pair = pair + second + shifted(second)
    updated = (
        previous + AGE_STEP * 0.25 * pair - (extended - 2.0 * previous + shifted(previous)) / 6.0
    )
    results[1] = jnp.where(kept, extended, updated)[:, 2 * FIL :]
    send_updated = [
        pltpu.make_async_copy(results.at[1, i : i + 1], updated_ref.at[i], semaphores.at[1, i])
        for i in range(3)
    ]
    for copy in send_updated:
        copy.start()
    for copy in send_first + send_updated:
        copy.wait()


def buffers(wakes, segs):
    shapes = ((TERMS, segs), BF16), ((SUMS, segs), BF16), ((1, segs), F32)
    return [((wakes, *shape), dtype) for shape, dtype in shapes]


def outs(*specs):
    return tuple(jax.ShapeDtypeStruct(shape, dtype) for shape, dtype in specs)


def cost(points, segs):
    pairs = points * segs
    return pl.CostEstimate(flops=500 * pairs, bytes_accessed=400 * segs, transcendentals=3 * pairs)


def local(nodes, segments, circulation, upstream, upstream_mask):
    rows, bands = lax.axis_size("row"), lax.axis_size("band")
    group = min(8, rows // 2)
    seg_count = segments.shape[2]
    count = nodes.shape[2]
    points = count + 2 * FIL
    sums = ((SUMS, points), F32)

    own = pl.pallas_call(
        pack_kernel,
        out_shape=pltpu.VMEM((8, seg_count), F32),
        in_specs=[ANY] * 3,
        out_specs=VMEM,
        scratch_shapes=[pltpu.SemaphoreType.DMA((10,))],
    )(nodes.transpose(1, 0, 2), segments.transpose(1, 0, 2), circulation)[None]

    low, parts = group // 2, bands // 2
    tops = group // low

    def permuted(blocks, target):
        route = [(i * bands + j, target(i, j)) for i in range(rows) for j in range(bands)]
        return lax.ppermute(blocks, ("row", "band"), route)

    def flipped(blocks, row_flip, band_flip):
        return permuted(blocks, lambda i, j: (i ^ row_flip) * bands + (j ^ band_flip))

    behind = permuted(own, lambda i, j: i * bands + (j + 1) % bands)
    near = [
        permuted(own, lambda i, j: ((i ^ flip) + group) % rows * bands + j)
        for flip in range(0, group, low)
    ]
    extended, factors, *wake_own, total = pl.pallas_call(
        functools.partial(own_kernel, count),
        out_shape=outs(
            ((3, points), F32), ((2 * points, TERMS), BF16), *buffers(1, 3 * seg_count), sums
        ),
        in_specs=[VMEM] * 2,
        out_specs=(VMEM,) * 6,
        compiler_params=PARAMS,
        cost_estimate=cost(points, 2 * seg_count),
    )(own, behind)

    *near, total = lax.optimization_barrier((*near, total))
    near = jnp.concatenate(near)
    with_own = flipped(jnp.concatenate([near, own]), 0, 2)
    far = [with_own[:tops]] + [
        flipped(near, row_flip, 2 * band_flip) for row_flip in range(1, low) for band_flip in range(parts)
    ]
    *listed, total = pl.pallas_call(
        functools.partial(near_kernel, group),
        out_shape=outs(*buffers(LISTED, parts * seg_count), sums),
        in_specs=[VMEM] * 5,
        out_specs=(VMEM,) * 4,
        compiler_params=PARAMS,
        cost_estimate=cost(points, LISTED * seg_count),
    )(upstream, upstream_mask, near, factors, total)
    *far, with_own, total = lax.optimization_barrier((*far, with_own, total))
    far, across = jnp.concatenate(far), with_own[tops:]
    last = flipped(jnp.concatenate([near, far, own, across]), 0, 1)
    held = outs(*buffers(LISTED, parts * seg_count), *buffers(1, 3 * seg_count), sums)
    *held, total = pl.pallas_call(
        functools.partial(far_kernel, group, parts),
        out_shape=held,
        in_specs=[VMEM] * 12,
        out_specs=(VMEM,) * 7,
        input_output_aliases={6 + i: i for i in range(6)},
        compiler_params=PARAMS,
        cost_estimate=cost(points, LISTED * seg_count),
    )(upstream, upstream_mask, far, across, factors, total, *listed, *wake_own)

    out = ((3, 1, count), F32)
    updated, first = pl.pallas_call(
        functools.partial(last_kernel, group, parts),
        out_shape=outs(out, out),
        in_specs=[VMEM] * 12,
        out_specs=(ANY,) * 2,
        scratch_shapes=[
            *[pltpu.VMEM(shape, dtype) for shape, dtype in buffers(LISTED, parts * seg_count)],
            *[pltpu.VMEM(shape, dtype) for shape, dtype in buffers(1, seg_count)],
            pltpu.VMEM((2, 3, count), F32),
            pltpu.SemaphoreType.DMA((2, 3)),
        ],
        compiler_params=PARAMS,
        cost_estimate=cost(points, 4 * bands * seg_count),
    )(upstream, upstream_mask, last, extended, factors, total, *held[3:], *held[:3])
    return updated.transpose(1, 0, 2), first.transpose(1, 0, 2)


def solution(mesh):
    placed = (
        P("row", None, "band"),
        P("row", None, "band"),
        P("row", "band"),
        P("row", None),
        P("row", None),
    )
    return jax.shard_map(
        local,
        mesh=mesh,
        in_specs=placed,
        out_specs=(P("row", None, "band"), P("row", None, "band")),
        check_vma=False,
    )
```

```python
import functools
import math

import jax
import jax.numpy as jnp
from jax import lax
from jax.experimental import pallas as pl
from jax.experimental.pallas import tpu as pltpu
from jax.sharding import PartitionSpec as P

FIL = 8
CORE_SQUARE = 0.04
AGE_STEP = 0.25
LISTED = 3
TILE = 256
TERMS = 96
SUMS = 32
F32, BF16 = jnp.float32, jnp.bfloat16
VMEM = pl.BlockSpec(memory_space=pltpu.VMEM)
ANY = pl.BlockSpec(memory_space=pl.ANY)
PARAMS = pltpu.CompilerParams(vmem_limit_bytes=32 * 2**20)


def split(value):
    high = value.astype(BF16).astype(F32)
    rest = value - high
    middle = rest.astype(BF16).astype(F32)
    return high, middle, rest - middle


def point_factors(points):
    count = points.shape[1]
    zeros = lambda rows: jnp.zeros((rows, count), F32)
    terms = split(-2.0 * points)
    squared = split(jnp.sum(points * points, axis=0, keepdims=True))
    one = jnp.ones((1, count), F32)
    both = []
    for end in (False, True):
        rows = []
        for term in (0, 1, 2, 0, 1, 2, 0, 1):
            rows += [zeros(3), terms[term], zeros(2)] if end else [terms[term], zeros(5)]
        for _ in range(3):
            rows += [zeros(1), one, zeros(6)] if end else [one, zeros(7)]
        rows += [*squared, zeros(5)]
        both.append(jnp.concatenate(rows, axis=0).T.astype(BF16))
    return jnp.concatenate(both, axis=0)


def segment_factors(block):
    one = jnp.ones((1, block.shape[1]), F32)
    zero = jnp.zeros_like(one)
    start = [block[i : i + 1] for i in range(3)]
    end = [block[i : i + 1] for i in range(3, 6)]
    scale = block[6:7] * (0.5 / math.pi)
    along = [a - b for a, b in zip(start, end)]
    moment = [
        start[1] * end[2] - start[2] * end[1],
        start[2] * end[0] - start[0] * end[2],
        start[0] * end[1] - start[1] * end[0],
    ]
    square = lambda v: v[0] * v[0] + v[1] * v[1] + v[2] * v[2]
    norms = jnp.concatenate(
        [square(start) + CORE_SQUARE, square(end) + CORE_SQUARE] + [zero] * 6, axis=0
    )
    high, middle, low = split(block)
    constant = jnp.concatenate([one] * 3 + [zero] * 5, axis=0)
    distance = jnp.concatenate(
        [high, high, high, middle, middle, middle, low, low, *split(norms), constant], axis=0
    ).astype(BF16)
    weights = jnp.concatenate([scale * v for v in along + moment] + [zero] * 2, axis=0)
    cross = jnp.concatenate([*split(weights), jnp.zeros_like(weights)], axis=0).astype(BF16)
    return distance, cross, square(along) + 2.0 * CORE_SQUARE


def add_tile(factors, distance, cross, length, total):
    points = factors.shape[0] // 2
    squared = jnp.dot(factors, distance, preferred_element_type=F32)
    squared_one, squared_two = squared[:points], squared[points:]
    inverse_one, inverse_two = lax.rsqrt(squared_one), lax.rsqrt(squared_two)
    norms = squared_one * inverse_one + squared_two * inverse_two
    factor = (inverse_one + inverse_two) * pltpu.reciprocal(norms * norms - length, approx=True)
    high = factor.astype(BF16)
    low = (factor - high.astype(F32)).astype(BF16)
    contract = (((1,), (1,)), ((), ()))
    return (
        total
        + lax.dot_general(cross, high, contract, preferred_element_type=F32)
        + lax.dot_general(cross, low, contract, preferred_element_type=F32)
    )


def view_of(buffers, wake, part, size):
    return tuple(ref.at[wake, :, part * size : (part + 1) * size] for ref in buffers)


def add_prepared(factors, view, total):
    distance, cross, length = view
    for tile in range(distance.shape[1] // TILE):
        at = pl.ds(tile * TILE, TILE)
        total = add_tile(factors, distance[:, at], cross[:, at], length[:, at], total)
    return total


def add_part(factors, block, view, total):
    for ref, value in zip(view, segment_factors(block)):
        ref[...] = value
    return add_prepared(factors, view, total)


def for_used(mask, branch, total):
    used = jnp.sum(mask[...])
    run = branch(0)
    for n in range(1, LISTED + 1):
        run = functools.partial(lambda n, low, high, t: lax.cond(used < n, low, high, t), n, run, branch(n))
    return run(total)


def slot_of(upstream, wake, group):
    lane = lax.broadcasted_iota(jnp.int32, upstream.shape, 1)
    listed = jnp.sum(jnp.where(lane == wake, upstream[...], 0))
    return lax.rem(listed, group) ^ lax.rem(lax.axis_index("row"), group)


def velocity(where_at, total):
    sums = total[0:8] + total[8:16] + total[16:24]
    x, y, z = where_at[0:1], where_at[1:2], where_at[2:3]
    dx, dy, dz = sums[0:1], sums[1:2], sums[2:3]
    return jnp.concatenate(
        [
            y * dz - z * dy + sums[3:4] + 1.0,
            z * dx - x * dz + sums[4:5],
            x * dy - y * dx + sums[5:6],
        ],
        axis=0,
    )


def pack_kernel(nodes, segments, circulation, packed, semaphores):
    count = nodes.shape[2]
    copies = [
        (circulation, packed.at[6:7]),
        *[(segments.at[i], packed.at[i : i + 1]) for i in range(6)],
        *[(nodes.at[i], packed.at[7:8, i * count : (i + 1) * count]) for i in range(3)],
    ]
    packed[7:8] = jnp.zeros((1, packed.shape[1]), F32)
    started = [
        pltpu.make_async_copy(source, target, semaphores.at[i])
        for i, (source, target) in enumerate(copies)
    ]
    for copy in started:
        copy.start()
    for copy in started:
        copy.wait()


def own_kernel(count, own, behind, ahead, extended_ref, factors_ref, distance, cross, length, total_ref):
    node_block = lambda block: jnp.concatenate(
        [block[7:8, i * count : (i + 1) * count] for i in range(3)], axis=0
    )
    points = node_block(own[0])
    root = points[:, :FIL]
    at_start = lax.axis_index("band") == 0
    halo = jnp.where(
        at_start, jnp.concatenate([root, root], axis=1), node_block(behind[0])[:, -2 * FIL :]
    )
    extended = jnp.concatenate([halo, points], axis=1)
    extended_ref[...] = extended
    factors = point_factors(extended)
    factors_ref[...] = factors
    size = own.shape[2]
    total = jnp.zeros(total_ref.shape, F32)
    for part, block in enumerate((own, behind, ahead)):
        total = add_part(factors, block[0], view_of((distance, cross, length), 0, part, size), total)
    total_ref[...] = total


def far_kernel(group, parts, upstream, mask, far, own, factors_ref, before, *refs):
    low = group // 2
    tops = group // low
    listed, total_ref, wake_own = refs[3:6], refs[6], refs[7:10]
    factors = factors_ref[...]
    size = own.shape[2]

    def branch(used):
        def run(total):
            total = add_part(factors, own[0], view_of(wake_own, 0, 3, size), total)
            for wake in range(used):
                slot = slot_of(upstream, wake, group)
                for part in range(parts):
                    at = (lax.rem(slot, low) * parts + part) * tops + slot // low
                    view = view_of(listed, wake, part, size)
                    total = add_part(factors, far[at], view, total)
            return total

        return run

    total_ref[...] = for_used(mask, branch, before[...])


def last_kernel(group, parts, upstream, mask, blocks, extended_ref, factors_ref, before, *refs):
    own, earlier = refs[:3], refs[3:6]
    updated_ref, first_ref = refs[6:8]
    newest = refs[8:11]
    results, semaphores = refs[11:]
    low = group // 2
    tops = group // low
    size = blocks.shape[2]
    factors = factors_ref[...]

    def first_branch(used):
        def run(total):
            for wake in range(used):
                slot = slot_of(upstream, wake, group)
                for part in range(parts):
                    at = (lax.rem(slot, low) * parts + part) * tops + slot // low
                    view = view_of(newest, wake, part, size)
                    total = add_part(factors, blocks[at], view, total)
            return total

        return run

    extended = extended_ref[...]
    total = for_used(mask, first_branch, before[...])
    first = velocity(extended, total)
    results[0] = first[:, 2 * FIL :]
    send_first = [
        pltpu.make_async_copy(results.at[0, i : i + 1], first_ref.at[i], semaphores.at[0, i])
        for i in range(3)
    ]
    for copy in send_first:
        copy.start()

    def shifted(field):
        return jnp.concatenate([field[:, :FIL], field[:, :-FIL]], axis=1)

    lane = lax.broadcasted_iota(jnp.int32, extended.shape, 1)
    at_start = lax.axis_index("band") == 0
    kept = (lane < FIL) | (at_start & (lane >= 2 * FIL) & (lane < 3 * FIL))
    pair = first + shifted(first)
    previous = shifted(extended)
    predicted = jnp.where(kept, extended, previous + AGE_STEP * 0.5 * pair)
    moved = point_factors(predicted)

    def second_branch(used):
        def run(total):
            total = add_prepared(moved, view_of(own, 0, 0, own[0].shape[2]), total)
            for wake in range(used):
                for held in (earlier, newest):
                    total = add_prepared(moved, view_of(held, wake, 0, held[0].shape[2]), total)
            return total

        return run

    total = for_used(mask, second_branch, jnp.zeros_like(total))
    second = velocity(predicted, total)
    pair = pair + second + shifted(second)
    updated = (
        previous + AGE_STEP * 0.25 * pair - (extended - 2.0 * previous + shifted(previous)) / 6.0
    )
    results[1] = jnp.where(kept, extended, updated)[:, 2 * FIL :]
    send_updated = [
        pltpu.make_async_copy(results.at[1, i : i + 1], updated_ref.at[i], semaphores.at[1, i])
        for i in range(3)
    ]
    for copy in send_updated:
        copy.start()
    for copy in send_first + send_updated:
        copy.wait()


def buffers(wakes, segs):
    shapes = ((TERMS, segs), BF16), ((SUMS, segs), BF16), ((1, segs), F32)
    return [((wakes, *shape), dtype) for shape, dtype in shapes]


def outs(*specs):
    return tuple(jax.ShapeDtypeStruct(shape, dtype) for shape, dtype in specs)


def cost(points, segs):
    pairs = points * segs
    return pl.CostEstimate(flops=500 * pairs, bytes_accessed=400 * segs, transcendentals=3 * pairs)


def local(nodes, segments, circulation, upstream, upstream_mask):
    rows, bands = lax.axis_size("row"), lax.axis_size("band")
    group = min(8, rows // 2)
    seg_count = segments.shape[2]
    count = nodes.shape[2]
    points = count + 2 * FIL
    sums = ((SUMS, points), F32)

    own = pl.pallas_call(
        pack_kernel,
        out_shape=pltpu.VMEM((8, seg_count), F32),
        in_specs=[ANY] * 3,
        out_specs=VMEM,
        scratch_shapes=[pltpu.SemaphoreType.DMA((10,))],
    )(nodes.transpose(1, 0, 2), segments.transpose(1, 0, 2), circulation)[None]

    low, parts = group // 2, bands // 2
    tops = group // low

    def permuted(blocks, target):
        route = [(i * bands + j, target(i, j)) for i in range(rows) for j in range(bands)]
        return lax.ppermute(blocks, ("row", "band"), route)

    def flipped(blocks, row_flip, band_flip):
        return permuted(blocks, lambda i, j: (i ^ row_flip) * bands + (j ^ band_flip))

    behind = permuted(own, lambda i, j: i * bands + (j + 1) % bands)
    ahead = permuted(own, lambda i, j: i * bands + (j - 1) % bands)
    near = [
        permuted(own, lambda i, j: ((i ^ flip) + group) % rows * bands + j)
        for flip in range(0, group, low)
    ]
    extended, factors, *wake_own, total = pl.pallas_call(
        functools.partial(own_kernel, count),
        out_shape=outs(
            ((3, points), F32), ((2 * points, TERMS), BF16), *buffers(1, bands * seg_count), sums
        ),
        in_specs=[VMEM] * 3,
        out_specs=(VMEM,) * 6,
        compiler_params=PARAMS,
        cost_estimate=cost(points, 3 * seg_count),
    )(own, behind, ahead)

    *near, total = lax.optimization_barrier((*near, total))
    near = jnp.concatenate(near)
    with_own = flipped(jnp.concatenate([near, own]), 0, 2)
    far = [near, with_own[:tops]] + [
        flipped(near, row_flip, 2 * band_flip) for row_flip in range(1, low) for band_flip in range(parts)
    ]
    far = jnp.concatenate(far)
    last = flipped(far, 0, 1)
    *listed, total, d, c, e = pl.pallas_call(
        functools.partial(far_kernel, group, parts),
        out_shape=outs(*buffers(LISTED, parts * seg_count), sums, *buffers(1, bands * seg_count)),
        in_specs=[VMEM] * 9,
        out_specs=(VMEM,) * 7,
        input_output_aliases={6 + i: 4 + i for i in range(3)},
        compiler_params=PARAMS,
        cost_estimate=cost(points, LISTED * seg_count),
    )(upstream, upstream_mask, far, with_own[tops:], factors, total, *wake_own)
    wake_own = d, c, e

    out = ((3, 1, count), F32)
    updated, first = pl.pallas_call(
        functools.partial(last_kernel, group, parts),
        out_shape=outs(out, out),
        in_specs=[VMEM] * 12,
        out_specs=(ANY,) * 2,
        scratch_shapes=[
            *[pltpu.VMEM(shape, dtype) for shape, dtype in buffers(LISTED, parts * seg_count)],
            pltpu.VMEM((2, 3, count), F32),
            pltpu.SemaphoreType.DMA((2, 3)),
        ],
        compiler_params=PARAMS,
        cost_estimate=cost(points, 4 * bands * seg_count),
    )(upstream, upstream_mask, last, extended, factors, total, *wake_own, *listed)
    return updated.transpose(1, 0, 2), first.transpose(1, 0, 2)


def solution(mesh):
    placed = (
        P("row", None, "band"),
        P("row", None, "band"),
        P("row", "band"),
        P("row", None),
        P("row", None),
    )
    return jax.shard_map(
        local,
        mesh=mesh,
        in_specs=placed,
        out_specs=(P("row", None, "band"), P("row", None, "band")),
        check_vma=False,
    )
```

```python
import functools
import math

import jax
import jax.numpy as jnp
from jax import lax
from jax.experimental import pallas as pl
from jax.experimental.pallas import tpu as pltpu
from jax.sharding import PartitionSpec as P

FIL = 8
CORE_SQUARE = 0.04
AGE_STEP = 0.25
LISTED = 3
TILE = 256
TERMS = 96
SUMS = 32
F32, BF16 = jnp.float32, jnp.bfloat16
VMEM = pl.BlockSpec(memory_space=pltpu.VMEM)
ANY = pl.BlockSpec(memory_space=pl.ANY)
PARAMS = pltpu.CompilerParams(vmem_limit_bytes=32 * 2**20)


def split(value):
    high = value.astype(BF16).astype(F32)
    rest = value - high
    middle = rest.astype(BF16).astype(F32)
    return high, middle, rest - middle


def point_factors(points):
    count = points.shape[1]
    zeros = lambda rows: jnp.zeros((rows, count), F32)
    terms = split(-2.0 * points)
    squared = split(jnp.sum(points * points, axis=0, keepdims=True))
    one = jnp.ones((1, count), F32)
    both = []
    for end in (False, True):
        rows = []
        for term in (0, 1, 2, 0, 1, 2, 0, 1):
            rows += [zeros(3), terms[term], zeros(2)] if end else [terms[term], zeros(5)]
        for _ in range(3):
            rows += [zeros(1), one, zeros(6)] if end else [one, zeros(7)]
        rows += [*squared, zeros(5)]
        both.append(jnp.concatenate(rows, axis=0).T.astype(BF16))
    return jnp.concatenate(both, axis=0)


def segment_factors(block):
    one = jnp.ones((1, block.shape[1]), F32)
    zero = jnp.zeros_like(one)
    start = [block[i : i + 1] for i in range(3)]
    end = [block[i : i + 1] for i in range(3, 6)]
    scale = block[6:7] * (0.5 / math.pi)
    along = [a - b for a, b in zip(start, end)]
    moment = [
        start[1] * end[2] - start[2] * end[1],
        start[2] * end[0] - start[0] * end[2],
        start[0] * end[1] - start[1] * end[0],
    ]
    square = lambda v: v[0] * v[0] + v[1] * v[1] + v[2] * v[2]
    norms = jnp.concatenate(
        [square(start) + CORE_SQUARE, square(end) + CORE_SQUARE] + [zero] * 6, axis=0
    )
    high, middle, low = split(block)
    constant = jnp.concatenate([one] * 3 + [zero] * 5, axis=0)
    distance = jnp.concatenate(
        [high, high, high, middle, middle, middle, low, low, *split(norms), constant], axis=0
    ).astype(BF16)
    weights = jnp.concatenate([scale * v for v in along + moment] + [zero] * 2, axis=0)
    cross = jnp.concatenate([*split(weights), jnp.zeros_like(weights)], axis=0).astype(BF16)
    return distance, cross, square(along) + 2.0 * CORE_SQUARE


def add_tile(factors, distance, cross, length, total):
    points = factors.shape[0] // 2
    squared = jnp.dot(factors, distance, preferred_element_type=F32)
    squared_one, squared_two = squared[:points], squared[points:]
    inverse_one, inverse_two = lax.rsqrt(squared_one), lax.rsqrt(squared_two)
    norms = squared_one * inverse_one + squared_two * inverse_two
    factor = (inverse_one + inverse_two) * pltpu.reciprocal(norms * norms - length, approx=True)
    high = factor.astype(BF16)
    low = (factor - high.astype(F32)).astype(BF16)
    contract = (((1,), (1,)), ((), ()))
    return (
        total
        + lax.dot_general(cross, high, contract, preferred_element_type=F32)
        + lax.dot_general(cross, low, contract, preferred_element_type=F32)
    )


def view_of(buffers, index):
    return tuple(ref.at[index] for ref in buffers)


def add_prepared(factors, view, total):
    distance, cross, length = view
    for tile in range(distance.shape[1] // TILE):
        at = pl.ds(tile * TILE, TILE)
        total = add_tile(factors, distance[:, at], cross[:, at], length[:, at], total)
    return total


def add_part(factors, block, view, total):
    for ref, value in zip(view, segment_factors(block)):
        ref[...] = value
    return add_prepared(factors, view, total)


def for_count(count, most, branch, total):
    run = branch(0)
    for n in range(1, most + 1):
        run = functools.partial(
            lambda n, low, high, t: lax.cond(count < n, low, high, t), n, run, branch(n)
        )
    return run(total)


def used_wakes(plan):
    return jnp.sum(plan[1:2, :])


def slot_of(plan, wake, group):
    listed = jnp.sum(plan[0:1, wake : wake + 1])
    return lax.rem(listed, group) ^ lax.rem(lax.axis_index("row"), group)


def velocity(where_at, total):
    sums = total[0:8] + total[8:16] + total[16:24]
    x, y, z = where_at[0:1], where_at[1:2], where_at[2:3]
    dx, dy, dz = sums[0:1], sums[1:2], sums[2:3]
    return jnp.concatenate(
        [
            y * dz - z * dy + sums[3:4] + 1.0,
            z * dx - x * dz + sums[4:5],
            x * dy - y * dx + sums[5:6],
        ],
        axis=0,
    )


def pack_kernel(nodes, segments, circulation, packed, semaphores):
    count = nodes.shape[2]
    copies = [
        (circulation, packed.at[6:7]),
        *[(segments.at[i], packed.at[i : i + 1]) for i in range(6)],
        *[(nodes.at[i], packed.at[7:8, i * count : (i + 1) * count]) for i in range(3)],
    ]
    packed[7:8] = jnp.zeros((1, packed.shape[1]), F32)
    started = [
        pltpu.make_async_copy(source, target, semaphores.at[i])
        for i, (source, target) in enumerate(copies)
    ]
    for copy in started:
        copy.start()
    for copy in started:
        copy.wait()


def own_kernel(
    count, upstream, mask, own, behind, extended_ref, factors_ref, plan, distance, cross, length, total_ref
):
    plan[0:1, :] = upstream[...]
    plan[1:2, :] = mask[...]
    node_block = lambda block: jnp.concatenate(
        [block[7:8, i * count : (i + 1) * count] for i in range(3)], axis=0
    )
    points = node_block(own[0])
    root = points[:, :FIL]
    at_start = lax.axis_index("band") == 0
    halo = jnp.where(
        at_start, jnp.concatenate([root, root], axis=1), node_block(behind[0])[:, -2 * FIL :]
    )
    extended = jnp.concatenate([halo, points], axis=1)
    extended_ref[...] = extended
    factors = point_factors(extended)
    factors_ref[...] = factors
    total = jnp.zeros(total_ref.shape, F32)
    for part, block in enumerate((own, behind)):
        total = add_part(factors, block[0], view_of((distance, cross, length), part), total)
    total_ref[...] = total


def near_kernel(group, parts, plan, near, factors_ref, before, distance, cross, length, total_ref):
    low = group // 2
    used = used_wakes(plan)
    factors = factors_ref[...]
    total = before[...]
    for wake in range(LISTED):
        slot = slot_of(plan, wake, group)
        add = functools.partial(
            lambda at, view, total: add_part(factors, near[at], view, total),
            slot // low,
            view_of((distance, cross, length), wake * parts),
        )
        here = (wake < used) & (lax.rem(slot, low) == 0)
        total = lax.cond(here, add, lambda total: total, total)
    total_ref[...] = total


def far_kernel(group, parts, plan, far, own, factors_ref, before, *refs):
    low = group // 2
    tops = group // low
    listed, wake_own, total_ref = refs[6:9], refs[9:12], refs[12]
    factors = factors_ref[...]
    used = used_wakes(plan)
    most = LISTED * parts
    count = 0
    sources, targets = [0] * most, [0] * most
    for wake in range(LISTED):
        slot = slot_of(plan, wake, group)
        for part in range(parts):
            wanted = wake < used if part else (wake < used) & (lax.rem(slot, low) != 0)
            source = (lax.rem(slot, low) * parts + part) * tops + slot // low
            for item in range(wake * parts + part + 1):
                taken = wanted & (count == item)
                sources[item] = jnp.where(taken, source, sources[item])
                targets[item] = jnp.where(taken, wake * parts + part, targets[item])
            count = count + wanted.astype(jnp.int32)

    def branch(items):
        def run(total):
            total = add_part(factors, own[0], view_of(wake_own, 2), total)
            for item in range(items):
                view = view_of(listed, targets[item])
                total = add_part(factors, far[sources[item]], view, total)
            return total

        return run

    total_ref[...] = for_count(count, most, branch, before[...])


def last_kernel(group, parts, plan, blocks, extended_ref, factors_ref, before, *refs):
    own, earlier = refs[:3], refs[3:6]
    updated_ref, first_ref = refs[6:8]
    newest, newest_own = refs[8:11], refs[11:14]
    results, semaphores = refs[14:]
    low = group // 2
    tops = group // low
    factors = factors_ref[...]
    used = used_wakes(plan)
    slots = [slot_of(plan, wake, group) for wake in range(LISTED)]
    own_at = blocks.shape[0] - 2 + lax.rem(lax.axis_index("band"), 2)

    def first_branch(wakes):
        def run(total):
            total = add_part(factors, blocks[own_at], view_of(newest_own, 0), total)
            for wake in range(wakes):
                slot = slots[wake]
                for part in range(parts):
                    at = (lax.rem(slot, low) * parts + part) * tops + slot // low
                    view = view_of(newest, wake * parts + part)
                    total = add_part(factors, blocks[at], view, total)
            return total

        return run

    extended = extended_ref[...]
    total = for_count(used, LISTED, first_branch, before[...])
    first = velocity(extended, total)
    results[0] = first[:, 2 * FIL :]
    send_first = [
        pltpu.make_async_copy(results.at[0, i : i + 1], first_ref.at[i], semaphores.at[0, i])
        for i in range(3)
    ]
    for copy in send_first:
        copy.start()

    def shifted(field):
        return jnp.concatenate([field[:, :FIL], field[:, :-FIL]], axis=1)

    lane = lax.broadcasted_iota(jnp.int32, extended.shape, 1)
    at_start = lax.axis_index("band") == 0
    kept = (lane < FIL) | (at_start & (lane >= 2 * FIL) & (lane < 3 * FIL))
    pair = first + shifted(first)
    previous = shifted(extended)
    predicted = jnp.where(kept, extended, previous + AGE_STEP * 0.5 * pair)
    moved = point_factors(predicted)

    def second_branch(wakes):
        views = [view_of(own, part) for part in range(own[0].shape[0])] + [view_of(newest_own, 0)]
        for index in range(wakes * parts):
            views += [view_of(earlier, index), view_of(newest, index)]

        def run(total):
            for view in views:
                total = add_prepared(moved, view, total)
            return total

        return run

    total = for_count(used, LISTED, second_branch, jnp.zeros_like(total))
    second = velocity(predicted, total)
    pair = pair + second + shifted(second)
    updated = (
        previous + AGE_STEP * 0.25 * pair - (extended - 2.0 * previous + shifted(previous)) / 6.0
    )
    results[1] = jnp.where(kept, extended, updated)[:, 2 * FIL :]
    send_updated = [
        pltpu.make_async_copy(results.at[1, i : i + 1], updated_ref.at[i], semaphores.at[1, i])
        for i in range(3)
    ]
    for copy in send_updated:
        copy.start()
    for copy in send_first + send_updated:
        copy.wait()


def buffers(wakes, segs):
    shapes = ((TERMS, segs), BF16), ((SUMS, segs), BF16), ((1, segs), F32)
    return [((wakes, *shape), dtype) for shape, dtype in shapes]


def outs(*specs):
    return tuple(jax.ShapeDtypeStruct(shape, dtype) for shape, dtype in specs)


def cost(points, segs):
    pairs = points * segs
    return pl.CostEstimate(flops=500 * pairs, bytes_accessed=400 * segs, transcendentals=3 * pairs)


def local(nodes, segments, circulation, upstream, upstream_mask):
    rows, bands = lax.axis_size("row"), lax.axis_size("band")
    group = min(8, rows // 2)
    seg_count = segments.shape[2]
    count = nodes.shape[2]
    points = count + 2 * FIL
    sums = ((SUMS, points), F32)

    own = pl.pallas_call(
        pack_kernel,
        out_shape=pltpu.VMEM((8, seg_count), F32),
        in_specs=[ANY] * 3,
        out_specs=VMEM,
        scratch_shapes=[pltpu.SemaphoreType.DMA((10,))],
    )(nodes.transpose(1, 0, 2), segments.transpose(1, 0, 2), circulation)[None]

    low, parts = group // 2, bands // 2
    tops = group // low

    def permuted(blocks, target):
        route = [(i * bands + j, target(i, j)) for i in range(rows) for j in range(bands)]
        return lax.ppermute(blocks, ("row", "band"), route)

    def flipped(blocks, row_flip, band_flip):
        return permuted(blocks, lambda i, j: (i ^ row_flip) * bands + (j ^ band_flip))

    behind = permuted(own, lambda i, j: i * bands + (j + 1) % bands)
    near = [
        permuted(own, lambda i, j: ((i ^ flip) + group) % rows * bands + j)
        for flip in range(0, group, low)
    ]
    extended, factors, plan, *wake_own, total = pl.pallas_call(
        functools.partial(own_kernel, count),
        out_shape=outs(
            ((3, points), F32),
            ((2 * points, TERMS), BF16),
            ((2, LISTED), jnp.int32),
            *buffers(3, seg_count),
            sums,
        ),
        in_specs=[VMEM] * 4,
        out_specs=(VMEM,) * 7,
        compiler_params=PARAMS,
        cost_estimate=cost(points, 2 * seg_count),
    )(upstream, upstream_mask, own, behind)

    *near, total = lax.optimization_barrier((*near, total))
    near = jnp.concatenate(near)
    with_own = flipped(jnp.concatenate([near, own]), 0, 2)
    far = [with_own[:tops]] + [
        flipped(near, row_flip, 2 * band_flip) for row_flip in range(1, low) for band_flip in range(parts)
    ]
    *listed, total = pl.pallas_call(
        functools.partial(near_kernel, group, parts),
        out_shape=outs(*buffers(LISTED * parts, seg_count), sums),
        in_specs=[VMEM] * 4,
        out_specs=(VMEM,) * 4,
        compiler_params=PARAMS,
        cost_estimate=cost(points, LISTED * seg_count),
    )(plan, near, factors, total)
    *far, with_own, total = lax.optimization_barrier((*far, with_own, total))
    across = with_own[tops:]
    far = jnp.concatenate([near, *far, own, across])
    last = flipped(far, 0, 1)
    *held, total = pl.pallas_call(
        functools.partial(far_kernel, group, parts),
        out_shape=outs(*buffers(LISTED * parts, seg_count), *buffers(3, seg_count), sums),
        in_specs=[VMEM] * 11,
        out_specs=(VMEM,) * 7,
        input_output_aliases={5 + i: i for i in range(6)},
        compiler_params=PARAMS,
        cost_estimate=cost(points, LISTED * seg_count),
    )(plan, far, across, factors, total, *listed, *wake_own)
    listed, wake_own = held[:3], held[3:]

    out = ((3, 1, count), F32)
    updated, first = pl.pallas_call(
        functools.partial(last_kernel, group, parts),
        out_shape=outs(out, out),
        in_specs=[VMEM] * 11,
        out_specs=(ANY,) * 2,
        scratch_shapes=[
            *[pltpu.VMEM(shape, dtype) for shape, dtype in buffers(LISTED * parts, seg_count)],
            *[pltpu.VMEM(shape, dtype) for shape, dtype in buffers(1, seg_count)],
            pltpu.VMEM((2, 3, count), F32),
            pltpu.SemaphoreType.DMA((2, 3)),
        ],
        compiler_params=PARAMS,
        cost_estimate=cost(points, 4 * bands * seg_count),
    )(plan, last, extended, factors, total, *wake_own, *listed)
    return updated.transpose(1, 0, 2), first.transpose(1, 0, 2)


def solution(mesh):
    placed = (
        P("row", None, "band"),
        P("row", None, "band"),
        P("row", "band"),
        P("row", None),
        P("row", None),
    )
    return jax.shard_map(
        local,
        mesh=mesh,
        in_specs=placed,
        out_specs=(P("row", None, "band"), P("row", None, "band")),
        check_vma=False,
    )
```

```python
import functools
import math

import jax
import jax.numpy as jnp
from jax import lax
from jax.experimental import pallas as pl
from jax.experimental.pallas import tpu as pltpu
from jax.sharding import PartitionSpec as P

FIL = 8
CORE_SQUARE = 0.04
AGE_STEP = 0.25
LISTED = 3
TILE = 256
TERMS = 96
SUMS = 32
F32, BF16 = jnp.float32, jnp.bfloat16
VMEM = pl.BlockSpec(memory_space=pltpu.VMEM)
ANY = pl.BlockSpec(memory_space=pl.ANY)
PARAMS = pltpu.CompilerParams(vmem_limit_bytes=32 * 2**20)


def split(value):
    high = value.astype(BF16).astype(F32)
    rest = value - high
    middle = rest.astype(BF16).astype(F32)
    return high, middle, rest - middle


def point_factors(points):
    count = points.shape[1]
    zeros = lambda rows: jnp.zeros((rows, count), F32)
    terms = split(-2.0 * points)
    one = jnp.ones((1, count), F32)
    rows = []
    for term in (0, 1, 2, 0, 1, 2, 0, 1):
        rows += [terms[term], zeros(5)]
    rows += [one, zeros(7)] * 3
    rows += [*split(jnp.sum(points * points, axis=0, keepdims=True)), zeros(128 - TERMS + 5)]
    first = jnp.concatenate(rows, axis=0).T
    both = jnp.concatenate([first, pltpu.roll(first, 3, 1)], axis=0)
    return both[:, :TERMS].astype(BF16)


def segment_factors(block):
    one = jnp.ones((1, block.shape[1]), F32)
    zero = jnp.zeros_like(one)
    start = [block[i : i + 1] for i in range(3)]
    end = [block[i : i + 1] for i in range(3, 6)]
    scale = block[6:7] * (0.5 / math.pi)
    along = [a - b for a, b in zip(start, end)]
    moment = [
        start[1] * end[2] - start[2] * end[1],
        start[2] * end[0] - start[0] * end[2],
        start[0] * end[1] - start[1] * end[0],
    ]
    square = lambda v: v[0] * v[0] + v[1] * v[1] + v[2] * v[2]
    norms = jnp.concatenate(
        [square(start) + CORE_SQUARE, zero, zero, square(end) + CORE_SQUARE] + [zero] * 4, axis=0
    )
    high, middle, low = split(block)
    constant = jnp.concatenate([one] * 6 + [zero] * 2, axis=0)
    distance = jnp.concatenate(
        [high, high, high, middle, middle, middle, low, low, *split(norms), constant], axis=0
    ).astype(BF16)
    weights = jnp.concatenate([scale * v for v in along + moment] + [zero] * 2, axis=0)
    cross = jnp.concatenate([*split(weights), jnp.zeros_like(weights)], axis=0).astype(BF16)
    return distance, cross, square(along) + 2.0 * CORE_SQUARE


def add_tile(factors, distance, cross, length, total):
    points = factors.shape[0] // 2
    squared = jnp.dot(factors, distance, preferred_element_type=F32)
    squared_one, squared_two = squared[:points], squared[points:]
    inverse_one, inverse_two = lax.rsqrt(squared_one), lax.rsqrt(squared_two)
    norms = squared_one * inverse_one + squared_two * inverse_two
    factor = (inverse_one + inverse_two) * pltpu.reciprocal(norms * norms - length, approx=True)
    high = factor.astype(BF16)
    low = (factor - high.astype(F32)).astype(BF16)
    contract = (((1,), (1,)), ((), ()))
    return (
        total
        + lax.dot_general(cross, high, contract, preferred_element_type=F32)
        + lax.dot_general(cross, low, contract, preferred_element_type=F32)
    )


def view_of(buffers, index):
    return tuple(ref.at[index] for ref in buffers)


def add_prepared(factors, view, total):
    distance, cross, length = view
    for tile in range(distance.shape[1] // TILE):
        at = pl.ds(tile * TILE, TILE)
        total = add_tile(factors, distance[:, at], cross[:, at], length[:, at], total)
    return total


def add_part(factors, block, view, total):
    for ref, value in zip(view, segment_factors(block)):
        ref[...] = value
    return add_prepared(factors, view, total)


def for_count(count, most, branch, total):
    run = branch(0)
    for n in range(1, most + 1):
        run = functools.partial(
            lambda n, low, high, t: lax.cond(count < n, low, high, t), n, run, branch(n)
        )
    return run(total)


def used_wakes(plan):
    return jnp.sum(plan[1:2, :])


def slot_of(plan, wake, group):
    listed = jnp.sum(plan[0:1, wake : wake + 1])
    return lax.rem(listed, group) ^ lax.rem(lax.axis_index("row"), group)


def velocity(where_at, total):
    sums = total[0:8] + total[8:16] + total[16:24]
    x, y, z = where_at[0:1], where_at[1:2], where_at[2:3]
    dx, dy, dz = sums[0:1], sums[1:2], sums[2:3]
    return jnp.concatenate(
        [
            y * dz - z * dy + sums[3:4] + 1.0,
            z * dx - x * dz + sums[4:5],
            x * dy - y * dx + sums[5:6],
        ],
        axis=0,
    )


def pack_kernel(nodes, segments, circulation, packed, semaphores):
    count = nodes.shape[2]
    copies = [
        (circulation, packed.at[6:7]),
        (segments.at[:, 0], packed.at[0:6]),
        *[(nodes.at[i], packed.at[7:8, i * count : (i + 1) * count]) for i in range(3)],
    ]
    packed[7:8] = jnp.zeros((1, packed.shape[1]), F32)
    started = [
        pltpu.make_async_copy(source, target, semaphores.at[i])
        for i, (source, target) in enumerate(copies)
    ]
    for copy in started:
        copy.start()
    for copy in started:
        copy.wait()


def own_kernel(
    count, upstream, mask, own, behind, extended_ref, factors_ref, plan, distance, cross, length, total_ref
):
    plan[0:1, :] = upstream[...]
    plan[1:2, :] = mask[...]
    node_block = lambda block: jnp.concatenate(
        [block[7:8, i * count : (i + 1) * count] for i in range(3)], axis=0
    )
    points = node_block(own[0])
    root = points[:, :FIL]
    at_start = lax.axis_index("band") == 0
    halo = jnp.where(
        at_start, jnp.concatenate([root, root], axis=1), node_block(behind[0])[:, -2 * FIL :]
    )
    extended = jnp.concatenate([halo, points], axis=1)
    extended_ref[...] = extended
    factors = point_factors(extended)
    factors_ref[...] = factors
    total = jnp.zeros(total_ref.shape, F32)
    for part, block in enumerate((own, behind)):
        total = add_part(factors, block[0], view_of((distance, cross, length), part), total)
    total_ref[...] = total


def parts_kernel(group, parts, wanted, most, plan, blocks, factors_ref, before, *refs):
    low = group // 2
    total_ref = refs[-1]
    views = refs[len(refs) // 2 : -1]
    listed, wake_own = views[:3], views[3:]
    factors = factors_ref[...]
    used = used_wakes(plan)
    count = 0
    sources, targets = [0] * most, [0] * most
    for wake in range(LISTED):
        slot = slot_of(plan, wake, group)
        same = lax.rem(slot, low) == 0
        for part in range(parts):
            chosen, source = wanted(same, part, lax.rem(slot, low), slot // low)
            if chosen is None:
                continue
            taken = chosen & (wake < used)
            for item in range(most):
                here = taken & (count == item)
                sources[item] = jnp.where(here, source, sources[item])
                targets[item] = jnp.where(here, wake * parts + part, targets[item])
            count = count + taken.astype(jnp.int32)

    def branch(items):
        def run(total):
            if wake_own:
                total = add_part(factors, blocks[blocks.shape[0] - 1], view_of(wake_own, 2), total)
            for item in range(items):
                view = view_of(listed, targets[item])
                total = add_part(factors, blocks[sources[item]], view, total)
            return total

        return run

    total_ref[...] = for_count(count, most, branch, before[...])


def first_parts_kernel(group, parts, most, plan, blocks, factors_ref, before, *refs):
    wanted = lambda same, part, bits, top: (None, None) if part else (same, top)
    parts_kernel(group, parts, wanted, most, plan, blocks, factors_ref, before, *[None] * 3, *refs)


def last_kernel(group, parts, plan, blocks, extended_ref, factors_ref, before, *refs):
    own, earlier = refs[:3], refs[3:6]
    updated_ref, first_ref = refs[6:8]
    newest, newest_own = refs[8:11], refs[11:14]
    results, semaphores = refs[14:]
    low = group // 2
    tops = group // low
    factors = factors_ref[...]
    used = used_wakes(plan)
    slots = [slot_of(plan, wake, group) for wake in range(LISTED)]
    own_at = blocks.shape[0] - 2 + lax.rem(lax.axis_index("band"), 2)

    def first_branch(wakes):
        def run(total):
            total = add_part(factors, blocks[own_at], view_of(newest_own, 0), total)
            for wake in range(wakes):
                slot = slots[wake]
                for part in range(parts):
                    at = (lax.rem(slot, low) * parts + part) * tops + slot // low
                    view = view_of(newest, wake * parts + part)
                    total = add_part(factors, blocks[at], view, total)
            return total

        return run

    extended = extended_ref[...]
    total = for_count(used, LISTED, first_branch, before[...])
    first = velocity(extended, total)
    results[0] = first[:, 2 * FIL :]
    send_first = [
        pltpu.make_async_copy(results.at[0, i : i + 1], first_ref.at[i], semaphores.at[0, i])
        for i in range(3)
    ]
    for copy in send_first:
        copy.start()

    def shifted(field):
        return jnp.concatenate([field[:, :FIL], field[:, :-FIL]], axis=1)

    lane = lax.broadcasted_iota(jnp.int32, extended.shape, 1)
    at_start = lax.axis_index("band") == 0
    kept = (lane < FIL) | (at_start & (lane >= 2 * FIL) & (lane < 3 * FIL))
    pair = first + shifted(first)
    previous = shifted(extended)
    predicted = jnp.where(kept, extended, previous + AGE_STEP * 0.5 * pair)
    moved = point_factors(predicted)

    def second_branch(wakes):
        views = [view_of(own, part) for part in range(own[0].shape[0])] + [view_of(newest_own, 0)]
        for index in range(wakes * parts):
            views += [view_of(earlier, index), view_of(newest, index)]

        def run(total):
            for view in views:
                total = add_prepared(moved, view, total)
            return total

        return run

    total = for_count(used, LISTED, second_branch, jnp.zeros_like(total))
    second = velocity(predicted, total)
    pair = pair + second + shifted(second)
    updated = (
        previous + AGE_STEP * 0.25 * pair - (extended - 2.0 * previous + shifted(previous)) / 6.0
    )
    results[1] = jnp.where(kept, extended, updated)[:, 2 * FIL :]
    send_updated = [
        pltpu.make_async_copy(results.at[1, i : i + 1], updated_ref.at[i], semaphores.at[1, i])
        for i in range(3)
    ]
    for copy in send_updated:
        copy.start()
    for copy in send_first + send_updated:
        copy.wait()


def buffers(wakes, segs):
    shapes = ((TERMS, segs), BF16), ((SUMS, segs), BF16), ((1, segs), F32)
    return [((wakes, *shape), dtype) for shape, dtype in shapes]


def outs(*specs):
    return tuple(jax.ShapeDtypeStruct(shape, dtype) for shape, dtype in specs)


def cost(points, segs):
    pairs = points * segs
    return pl.CostEstimate(flops=500 * pairs, bytes_accessed=400 * segs, transcendentals=3 * pairs)


def local(nodes, segments, circulation, upstream, upstream_mask):
    rows, bands = lax.axis_size("row"), lax.axis_size("band")
    group = min(8, rows // 2)
    seg_count = segments.shape[2]
    count = nodes.shape[2]
    points = count + 2 * FIL
    sums = ((SUMS, points), F32)

    own = pl.pallas_call(
        pack_kernel,
        out_shape=pltpu.VMEM((8, seg_count), F32),
        in_specs=[ANY] * 3,
        out_specs=VMEM,
        scratch_shapes=[pltpu.SemaphoreType.DMA((5,))],
    )(nodes.transpose(1, 0, 2), segments.transpose(1, 0, 2), circulation)[None]

    low, parts = group // 2, bands // 2
    tops = group // low

    def permuted(blocks, target):
        route = [(i * bands + j, target(i, j)) for i in range(rows) for j in range(bands)]
        return lax.ppermute(blocks, ("row", "band"), route)

    def flipped(blocks, row_flip, band_flip):
        return permuted(blocks, lambda i, j: (i ^ row_flip) * bands + (j ^ band_flip))

    behind = permuted(own, lambda i, j: i * bands + (j + 1) % bands)
    near = [
        permuted(own, lambda i, j: ((i ^ flip) + group) % rows * bands + j)
        for flip in range(0, group, low)
    ]
    extended, factors, plan, *wake_own, total = pl.pallas_call(
        functools.partial(own_kernel, count),
        out_shape=outs(
            ((3, points), F32),
            ((2 * points, TERMS), BF16),
            ((2, LISTED), jnp.int32),
            *buffers(3, seg_count),
            sums,
        ),
        in_specs=[VMEM] * 4,
        out_specs=(VMEM,) * 7,
        compiler_params=PARAMS,
        cost_estimate=cost(points, 2 * seg_count),
    )(upstream, upstream_mask, own, behind)

    def add_parts(wanted, most, blocks, total, held):
        *held, total = pl.pallas_call(
            functools.partial(parts_kernel, group, parts, wanted, most),
            out_shape=outs(*[(array.shape, array.dtype) for array in held], sums),
            in_specs=[VMEM] * (4 + len(held)),
            out_specs=(VMEM,) * (1 + len(held)),
            input_output_aliases={4 + i: i for i in range(len(held))},
            compiler_params=PARAMS,
            cost_estimate=cost(points, LISTED * seg_count),
        )(plan, blocks, factors, total, *held)
        return held, total

    *near, total = lax.optimization_barrier((*near, total))
    near = jnp.concatenate(near)
    with_own = flipped(jnp.concatenate([near, own]), 0, 2)
    far = [
        flipped(near, row_flip, 2 * band_flip) for row_flip in range(1, low) for band_flip in range(parts)
    ]
    some = min(LISTED, tops)
    *listed, total = pl.pallas_call(
        functools.partial(first_parts_kernel, group, parts, some),
        out_shape=outs(*buffers(LISTED * parts, seg_count), sums),
        in_specs=[VMEM] * 4,
        out_specs=(VMEM,) * 4,
        compiler_params=PARAMS,
        cost_estimate=cost(points, LISTED * seg_count),
    )(plan, near, factors, total)

    def brought_across(same, part, bits, top):
        return (same, (part - 1) * tops + top) if part else (None, None)

    def brought_along(same, part, bits, top):
        return ~same, (bits * parts + part) * tops + top

    with_own, total = lax.optimization_barrier((with_own, total))
    held, total = add_parts(
        brought_across, some * (parts - 1), with_own, total, [*listed, *wake_own]
    )
    listed, wake_own = held[:3], held[3:]
    *far, total = lax.optimization_barrier((*far, total))
    far = jnp.concatenate([near, with_own[:tops], *far, own, with_own[tops:]])
    last = flipped(far, 0, 1)
    listed, total = add_parts(
        brought_along, min(LISTED, group - tops) * parts, far, total, listed
    )

    out = ((3, 1, count), F32)
    updated, first = pl.pallas_call(
        functools.partial(last_kernel, group, parts),
        out_shape=outs(out, out),
        in_specs=[VMEM] * 11,
        out_specs=(ANY,) * 2,
        scratch_shapes=[
            *[pltpu.VMEM(shape, dtype) for shape, dtype in buffers(LISTED * parts, seg_count)],
            *[pltpu.VMEM(shape, dtype) for shape, dtype in buffers(1, seg_count)],
            pltpu.VMEM((2, 3, count), F32),
            pltpu.SemaphoreType.DMA((2, 3)),
        ],
        compiler_params=PARAMS,
        cost_estimate=cost(points, 4 * bands * seg_count),
    )(plan, last, extended, factors, total, *wake_own, *listed)
    return updated.transpose(1, 0, 2), first.transpose(1, 0, 2)


def solution(mesh):
    placed = (
        P("row", None, "band"),
        P("row", None, "band"),
        P("row", "band"),
        P("row", None),
        P("row", None),
    )
    return jax.shard_map(
        local,
        mesh=mesh,
        in_specs=placed,
        out_specs=(P("row", None, "band"), P("row", None, "band")),
        check_vma=False,
    )
```

```python
import functools
import math

import jax
import jax.numpy as jnp
from jax import lax
from jax.experimental import pallas as pl
from jax.experimental.pallas import tpu as pltpu
from jax.sharding import PartitionSpec as P

FIL = 8
CORE_SQUARE = 0.04
AGE_STEP = 0.25
LISTED = 3
TILE = 256
TERMS = 96
SUMS = 32
F32, BF16 = jnp.float32, jnp.bfloat16
VMEM = pl.BlockSpec(memory_space=pltpu.VMEM)
ANY = pl.BlockSpec(memory_space=pl.ANY)
PARAMS = pltpu.CompilerParams(vmem_limit_bytes=32 * 2**20)


def split(value):
    high = value.astype(BF16).astype(F32)
    rest = value - high
    middle = rest.astype(BF16).astype(F32)
    return high, middle, rest - middle


def point_factors(points):
    count = points.shape[1]
    zeros = lambda rows: jnp.zeros((rows, count), F32)
    terms = split(-2.0 * points)
    one = jnp.ones((1, count), F32)
    rows = []
    for term in (0, 1, 2, 0, 1, 2, 0, 1):
        rows += [terms[term], zeros(5)]
    rows += [one, zeros(7)] * 3
    rows += [*split(jnp.sum(points * points, axis=0, keepdims=True)), zeros(128 - TERMS + 5)]
    first = jnp.concatenate(rows, axis=0).T
    both = jnp.concatenate([first, pltpu.roll(first, 3, 1)], axis=0)
    return both[:, :TERMS].astype(BF16)


def segment_factors(block):
    one = jnp.ones((1, block.shape[1]), F32)
    zero = jnp.zeros_like(one)
    start = [block[i : i + 1] for i in range(3)]
    end = [block[i : i + 1] for i in range(3, 6)]
    scale = block[6:7] * (0.5 / math.pi)
    along = [a - b for a, b in zip(start, end)]
    moment = [
        start[1] * end[2] - start[2] * end[1],
        start[2] * end[0] - start[0] * end[2],
        start[0] * end[1] - start[1] * end[0],
    ]
    square = lambda v: v[0] * v[0] + v[1] * v[1] + v[2] * v[2]
    norms = jnp.concatenate(
        [square(start) + CORE_SQUARE, zero, zero, square(end) + CORE_SQUARE] + [zero] * 4, axis=0
    )
    high, middle, low = split(block)
    constant = jnp.concatenate([one] * 6 + [zero] * 2, axis=0)
    distance = jnp.concatenate(
        [high, high, high, middle, middle, middle, low, low, *split(norms), constant], axis=0
    ).astype(BF16)
    weights = jnp.concatenate([scale * v for v in along + moment] + [zero] * 2, axis=0)
    cross = jnp.concatenate([*split(weights), jnp.zeros_like(weights)], axis=0).astype(BF16)
    return distance, cross, square(along) + 2.0 * CORE_SQUARE


def add_tile(factors, distance, cross, length, total):
    points = factors.shape[0] // 2
    squared = jnp.dot(factors, distance, preferred_element_type=F32)
    squared_one, squared_two = squared[:points], squared[points:]
    inverse_one, inverse_two = lax.rsqrt(squared_one), lax.rsqrt(squared_two)
    norms = squared_one * inverse_one + squared_two * inverse_two
    factor = (inverse_one + inverse_two) * pltpu.reciprocal(norms * norms - length, approx=True)
    high = factor.astype(BF16)
    low = (factor - high.astype(F32)).astype(BF16)
    contract = (((1,), (1,)), ((), ()))
    return (
        total
        + lax.dot_general(cross, high, contract, preferred_element_type=F32)
        + lax.dot_general(cross, low, contract, preferred_element_type=F32)
    )


def view_of(buffers, index):
    return tuple(ref.at[index] for ref in buffers)


def add_prepared(factors, view, total):
    distance, cross, length = view
    for tile in range(distance.shape[1] // TILE):
        at = pl.ds(tile * TILE, TILE)
        total = add_tile(factors, distance[:, at], cross[:, at], length[:, at], total)
    return total


def add_part(factors, block, view, total):
    for ref, value in zip(view, segment_factors(block)):
        ref[...] = value
    return add_prepared(factors, view, total)


def for_count(count, most, branch, total):
    run = branch(0)
    for n in range(1, most + 1):
        run = functools.partial(
            lambda n, low, high, t: lax.cond(count < n, low, high, t), n, run, branch(n)
        )
    return run(total)


def used_wakes(plan):
    return jnp.sum(plan[1:2, :])


def slot_of(plan, wake, group):
    listed = jnp.sum(plan[0:1, wake : wake + 1])
    return lax.rem(listed, group) ^ lax.rem(lax.axis_index("row"), group)


def velocity(where_at, total):
    sums = total[0:8] + total[8:16] + total[16:24]
    x, y, z = where_at[0:1], where_at[1:2], where_at[2:3]
    dx, dy, dz = sums[0:1], sums[1:2], sums[2:3]
    return jnp.concatenate(
        [
            y * dz - z * dy + sums[3:4] + 1.0,
            z * dx - x * dz + sums[4:5],
            x * dy - y * dx + sums[5:6],
        ],
        axis=0,
    )


def pack_kernel(nodes, segments, circulation, packed, semaphores):
    count = nodes.shape[2]
    copies = [
        (circulation, packed.at[6:7]),
        (segments.at[:, 0], packed.at[0:6]),
        *[(nodes.at[i], packed.at[7:8, i * count : (i + 1) * count]) for i in range(3)],
    ]
    packed[7:8] = jnp.zeros((1, packed.shape[1]), F32)
    started = [
        pltpu.make_async_copy(source, target, semaphores.at[i])
        for i, (source, target) in enumerate(copies)
    ]
    for copy in started:
        copy.start()
    for copy in started:
        copy.wait()


def own_kernel(
    count, upstream, mask, own, behind, extended_ref, factors_ref, plan, distance, cross, length, total_ref
):
    plan[0:1, :] = upstream[...]
    plan[1:2, :] = mask[...]
    node_block = lambda block: jnp.concatenate(
        [block[7:8, i * count : (i + 1) * count] for i in range(3)], axis=0
    )
    points = node_block(own[0])
    root = points[:, :FIL]
    at_start = lax.axis_index("band") == 0
    halo = jnp.where(
        at_start, jnp.concatenate([root, root], axis=1), node_block(behind[0])[:, -2 * FIL :]
    )
    extended = jnp.concatenate([halo, points], axis=1)
    extended_ref[...] = extended
    factors = point_factors(extended)
    factors_ref[...] = factors
    total = jnp.zeros(total_ref.shape, F32)
    for part, block in enumerate((own, behind)):
        total = add_part(factors, block[0], view_of((distance, cross, length), part), total)
    total_ref[...] = total


def parts_kernel(group, parts, wanted, most, own_part, plan, blocks, factors_ref, before, *refs):
    low = group // 2
    total_ref = refs[-1]
    views = refs[len(refs) // 2 : -1]
    listed, wake_own = views[:3], views[3:]
    factors = factors_ref[...]
    used = used_wakes(plan)
    count = 0
    sources, targets = [0] * most, [0] * most
    for wake in range(LISTED):
        slot = slot_of(plan, wake, group)
        same = lax.rem(slot, low) == 0
        for part in range(parts):
            chosen, source = wanted(same, part, lax.rem(slot, low), slot // low)
            if chosen is None:
                continue
            taken = chosen & (wake < used)
            for item in range(most):
                here = taken & (count == item)
                sources[item] = jnp.where(here, source, sources[item])
                targets[item] = jnp.where(here, wake * parts + part, targets[item])
            count = count + taken.astype(jnp.int32)

    def branch(items):
        def run(total):
            if wake_own:
                other = lax.rem(lax.axis_index("band"), 2) - 1 if own_part == 3 else 0
                block = blocks[blocks.shape[0] - 1 + other]
                total = add_part(factors, block, view_of(wake_own, own_part), total)
            for item in range(items):
                view = view_of(listed, targets[item])
                total = add_part(factors, blocks[sources[item]], view, total)
            return total

        return run

    total_ref[...] = for_count(count, most, branch, before[...])


def first_parts_kernel(group, parts, most, plan, blocks, factors_ref, before, *refs):
    wanted = lambda same, part, bits, top: (None, None) if part else (same, top)
    parts_kernel(group, parts, wanted, most, 0, plan, blocks, factors_ref, before, *[None] * 3, *refs)


def last_kernel(group, parts, plan, blocks, extended_ref, factors_ref, before, *refs):
    own, earlier = refs[:3], refs[3:6]
    updated_ref, first_ref = refs[6:8]
    newest = refs[8:11]
    results, semaphores = refs[11:]
    low = group // 2
    tops = group // low
    factors = factors_ref[...]
    used = used_wakes(plan)
    slots = [slot_of(plan, wake, group) for wake in range(LISTED)]

    def first_branch(wakes):
        def run(total):
            for wake in range(wakes):
                slot = slots[wake]
                for part in range(parts):
                    at = (lax.rem(slot, low) * parts + part) * tops + slot // low
                    view = view_of(newest, wake * parts + part)
                    total = add_part(factors, blocks[at], view, total)
            return total

        return run

    extended = extended_ref[...]
    total = for_count(used, LISTED, first_branch, before[...])
    first = velocity(extended, total)
    results[0] = first[:, 2 * FIL :]
    send_first = [
        pltpu.make_async_copy(results.at[0, i : i + 1], first_ref.at[i], semaphores.at[0, i])
        for i in range(3)
    ]
    for copy in send_first:
        copy.start()

    def shifted(field):
        return jnp.concatenate([field[:, :FIL], field[:, :-FIL]], axis=1)

    lane = lax.broadcasted_iota(jnp.int32, extended.shape, 1)
    at_start = lax.axis_index("band") == 0
    kept = (lane < FIL) | (at_start & (lane >= 2 * FIL) & (lane < 3 * FIL))
    pair = first + shifted(first)
    previous = shifted(extended)
    predicted = jnp.where(kept, extended, previous + AGE_STEP * 0.5 * pair)
    moved = point_factors(predicted)

    def second_branch(wakes):
        views = [view_of(own, part) for part in range(own[0].shape[0])]
        for index in range(wakes * parts):
            views += [view_of(earlier, index), view_of(newest, index)]

        def run(total):
            for view in views:
                total = add_prepared(moved, view, total)
            return total

        return run

    total = for_count(used, LISTED, second_branch, jnp.zeros_like(total))
    second = velocity(predicted, total)
    pair = pair + second + shifted(second)
    updated = (
        previous + AGE_STEP * 0.25 * pair - (extended - 2.0 * previous + shifted(previous)) / 6.0
    )
    results[1] = jnp.where(kept, extended, updated)[:, 2 * FIL :]
    send_updated = [
        pltpu.make_async_copy(results.at[1, i : i + 1], updated_ref.at[i], semaphores.at[1, i])
        for i in range(3)
    ]
    for copy in send_updated:
        copy.start()
    for copy in send_first + send_updated:
        copy.wait()


def buffers(wakes, segs):
    shapes = ((TERMS, segs), BF16), ((SUMS, segs), BF16), ((1, segs), F32)
    return [((wakes, *shape), dtype) for shape, dtype in shapes]


def outs(*specs):
    return tuple(jax.ShapeDtypeStruct(shape, dtype) for shape, dtype in specs)


def cost(points, segs):
    pairs = points * segs
    return pl.CostEstimate(flops=500 * pairs, bytes_accessed=400 * segs, transcendentals=3 * pairs)


def local(nodes, segments, circulation, upstream, upstream_mask):
    rows, bands = lax.axis_size("row"), lax.axis_size("band")
    group = min(8, rows // 2)
    seg_count = segments.shape[2]
    count = nodes.shape[2]
    points = count + 2 * FIL
    sums = ((SUMS, points), F32)

    own = pl.pallas_call(
        pack_kernel,
        out_shape=pltpu.VMEM((8, seg_count), F32),
        in_specs=[ANY] * 3,
        out_specs=VMEM,
        scratch_shapes=[pltpu.SemaphoreType.DMA((5,))],
    )(nodes.transpose(1, 0, 2), segments.transpose(1, 0, 2), circulation)[None]

    low, parts = group // 2, bands // 2
    tops = group // low

    def permuted(blocks, target):
        route = [(i * bands + j, target(i, j)) for i in range(rows) for j in range(bands)]
        return lax.ppermute(blocks, ("row", "band"), route)

    def flipped(blocks, row_flip, band_flip):
        return permuted(blocks, lambda i, j: (i ^ row_flip) * bands + (j ^ band_flip))

    behind = permuted(own, lambda i, j: i * bands + (j + 1) % bands)
    near = [
        permuted(own, lambda i, j: ((i ^ flip) + group) % rows * bands + j)
        for flip in range(0, group, low)
    ]
    extended, factors, plan, *wake_own, total = pl.pallas_call(
        functools.partial(own_kernel, count),
        out_shape=outs(
            ((3, points), F32),
            ((2 * points, TERMS), BF16),
            ((2, LISTED), jnp.int32),
            *buffers(bands, seg_count),
            sums,
        ),
        in_specs=[VMEM] * 4,
        out_specs=(VMEM,) * 7,
        compiler_params=PARAMS,
        cost_estimate=cost(points, 2 * seg_count),
    )(upstream, upstream_mask, own, behind)

    def add_parts(wanted, most, own_part, blocks, total, held):
        *held, total = pl.pallas_call(
            functools.partial(parts_kernel, group, parts, wanted, most, own_part),
            out_shape=outs(*[(array.shape, array.dtype) for array in held], sums),
            in_specs=[VMEM] * (4 + len(held)),
            out_specs=(VMEM,) * (1 + len(held)),
            input_output_aliases={4 + i: i for i in range(len(held))},
            compiler_params=PARAMS,
            cost_estimate=cost(points, LISTED * seg_count),
        )(plan, blocks, factors, total, *held)
        return held, total

    *near, total = lax.optimization_barrier((*near, total))
    near = jnp.concatenate(near)
    with_own = flipped(jnp.concatenate([near, own]), 0, 2)
    far = [
        flipped(near, row_flip, 2 * band_flip) for row_flip in range(1, low) for band_flip in range(parts)
    ]
    some = min(LISTED, tops)
    *listed, total = pl.pallas_call(
        functools.partial(first_parts_kernel, group, parts, some),
        out_shape=outs(*buffers(LISTED * parts, seg_count), sums),
        in_specs=[VMEM] * 4,
        out_specs=(VMEM,) * 4,
        compiler_params=PARAMS,
        cost_estimate=cost(points, LISTED * seg_count),
    )(plan, near, factors, total)

    def brought_across(same, part, bits, top):
        return (same, (part - 1) * tops + top) if part else (None, None)

    def brought_along(same, part, bits, top):
        return ~same, (bits * parts + part) * tops + top

    with_own, total = lax.optimization_barrier((with_own, total))
    early = flipped(jnp.concatenate([own, with_own[tops:]]), 0, 1)
    held, total = add_parts(
        brought_across, some * (parts - 1), 2, with_own, total, [*listed, *wake_own]
    )
    *far, early, total = lax.optimization_barrier((*far, early, total))
    far = jnp.concatenate([near, with_own[:tops], *far])
    last = flipped(far, 0, 1)
    held, total = add_parts(
        brought_along,
        min(LISTED, group - tops) * parts,
        3,
        jnp.concatenate([far, early]),
        total,
        held,
    )
    listed, wake_own = held[:3], held[3:]

    out = ((3, 1, count), F32)
    updated, first = pl.pallas_call(
        functools.partial(last_kernel, group, parts),
        out_shape=outs(out, out),
        in_specs=[VMEM] * 11,
        out_specs=(ANY,) * 2,
        scratch_shapes=[
            *[pltpu.VMEM(shape, dtype) for shape, dtype in buffers(LISTED * parts, seg_count)],
            pltpu.VMEM((2, 3, count), F32),
            pltpu.SemaphoreType.DMA((2, 3)),
        ],
        compiler_params=PARAMS,
        cost_estimate=cost(points, 4 * bands * seg_count),
    )(plan, last, extended, factors, total, *wake_own, *listed)
    return updated.transpose(1, 0, 2), first.transpose(1, 0, 2)


def solution(mesh):
    placed = (
        P("row", None, "band"),
        P("row", None, "band"),
        P("row", "band"),
        P("row", None),
        P("row", None),
    )
    return jax.shard_map(
        local,
        mesh=mesh,
        in_specs=placed,
        out_specs=(P("row", None, "band"), P("row", None, "band")),
        check_vma=False,
    )
```
